128 devices in a mesh: dp: 16 (over z, x_hi, core), expert: 8 (over y, x_lo).
Axes of the slice: x: 4 (x_hi: 2, x_lo: 2; x = x_hi * 2 + x_lo), y: 4, z: 4, core: 2. Of those that a mesh axis runs over, the one named last changes fastest.
Arguments:
- tokens: bfloat16 [16384, 3584], P(('dp', 'expert')), may hold values from -6 to 6
- grad_out: bfloat16 [16384, 3584], P(('dp', 'expert')), may hold values from -1.5 to 1.5
- routes: int32 [16384, 2], P(('dp', 'expert')), may hold values from 0 to 7, all different within a row; in each aligned block of 128 rows (0 to 127, 128 to 255, ...) at most 64 rows name the same one
- probs: bfloat16 [16384, 2], P(('dp', 'expert')), may hold values from 0.099609375 to 1
- w_gate: bfloat16 [8, 3584, 1024], P('expert'), may hold values from -0.09375 to 0.09375
- w_up: bfloat16 [8, 3584, 1024], P('expert'), may hold values from -0.09375 to 0.09375
- w_down: bfloat16 [8, 3584, 1024], P('expert'), may hold values from -0.1875 to 0.1875
Outputs:
- grad_tokens: bfloat16 [16384, 3584], P(('dp', 'expert'))
- grad_weights: bfloat16 [16384, 2], P(('dp', 'expert'))
- grad_gate: bfloat16 [8, 3584, 1024], P('expert', 'dp')
- grad_up: bfloat16 [8, 3584, 1024], P('expert', 'dp')
- grad_down: bfloat16 [8, 3584, 1024], P('expert', 'dp')
The draws below stay inside these ranges and needn't reach their ends.
Inputs may be any that keep to these rules, and one draw needn't show every extreme that they name: `routes`: each row names 2 different experts; within the rows of one device no expert is named by more than 64 rows, and some device has an expert named by exactly 64 rows.
All inputs are finite; a program needn't handle non-finite values.
Results may differ from the reference program's by a relative error of at most 0.017.
Values may be sent and summed in bfloat16 or wider, within the bound.
No kernel may reach another device: no remote copies, remote signals or barrier semaphores. Data moves between devices by JAX's collectives and lax.ppermute only.
A program may use at most 256 MiB of HBM per device.

```python
import math
import jax
import jax.numpy as jnp
import numpy as np
from jax import lax

D = 3584
FF = 1024
TOP = 2
TOK_DEV = 128
CAP = 64
EXPERTS = 8
TOKENS = 16384
N_DP = 16
N_EXPERT = 8


def block_levels(own_key, dims, shards, low, largest):
    loudness, own = 1.0, jax.random.fold_in(own_key, 6)
    for position, blocks in shards:
        draws = jnp.exp(jax.random.uniform(jax.random.fold_in(own, position), (blocks,), jnp.float32, low / len(shards), largest / len(shards)))
        loudness = loudness * jnp.repeat(draws, dims[position] // blocks).reshape([-1 if axis == position else 1 for axis in range(len(dims))])
    return loudness


def routed_block(key, own, number, rows, amount, top, bound, skew):
    ranking = jax.random.permutation(key, amount)
    crowded, usual = load_shares(amount, rows * top, bound, skew, True), load_shares(amount, rows * top, bound, skew, False)
    places = jnp.arange(amount)

    def named(sizes, rotation):
        used = int((sizes > 0).sum())
        fixed = max(1, used // 4)
        shifted = fixed + (places - fixed + rotation * (used - fixed)) % max(1, amount - fixed)
        return jnp.zeros((amount,), jnp.int32).at[ranking[jnp.where(places < fixed, places, shifted)]].set(jnp.asarray(sizes, jnp.int32))

    sizes = jnp.where(number % 4 == 0, named(crowded, number // 4), named(usual, number - number // 4 - 1))
    mixed = jax.random.permutation(jax.random.fold_in(own, 3), amount)
    giver, receiver = mixed[0:amount // 2 * 2:2], mixed[1:amount // 2 * 2:2]
    room = jnp.minimum(sizes[giver] - 1, bound - sizes[receiver]) // 2
    room = jnp.where((giver == ranking[0]) | (receiver == ranking[0]) | (sizes[receiver] == 0), 0, jnp.maximum(room, 0))
    shifted = jax.random.randint(jax.random.fold_in(own, 4), (amount // 2,), 0, 1 << 20) % (room + 1)
    sizes = sizes.at[giver].add(-shifted).at[receiver].add(shifted)
    members = jnp.searchsorted(jnp.cumsum(sizes), jnp.arange(rows * top), side="right").astype(jnp.int32)
    table = members.reshape(top, rows).T
    table = table[jax.random.permutation(jax.random.fold_in(own, 1), rows)]
    rotation = jax.random.randint(jax.random.fold_in(own, 2), (rows, 1), 0, top)
    return jnp.take_along_axis(table, (jnp.arange(top)[None, :] + rotation) % top, axis=1)


def load_shares(number_of, total, reach, slope, full):
    loads = [(1 << 20) // math.isqrt(standing ** slope) + 1 for standing in range(1, number_of + 1)]
    largest = reach if full else min(reach, max(-(-total // number_of), total * loads[0] // sum(loads)))
    least = 1 if total - largest >= number_of - 1 else 0
    counts, surplus = [largest] + [least] * (number_of - 1), total - largest - least * (number_of - 1)
    while surplus > 0:
        candidates = [i for i in range(1, number_of) if counts[i] < largest] or [i for i in range(1, number_of) if counts[i] < reach]
        pool, remaining = sum([loads[i] for i in candidates]), surplus
        for i in candidates:
            more = min(reach - counts[i], max(1, remaining * loads[i] // pool), surplus)
            counts[i] = counts[i] + more
            surplus = surplus - more
    return np.array(counts)


def noise(key, dims, width, limit, pieces=(), kind=jnp.bfloat16):
    drawn = jax.random.normal(key, dims, jnp.float32) * width
    if len(pieces) > 0:
        drawn = block_levels(key, dims, pieces, -0.22, 0.18) * drawn
    return jnp.clip(drawn, min=-limit, max=limit).astype(kind)


def setup_inputs(seed: int = 0) -> dict:
    key_list = jax.random.split(jax.random.key(seed), 8)
    tokens = noise(key_list[0], (TOKENS, D), 1.0, 6.0, ((0, 128),))
    grad_out = noise(key_list[1], (TOKENS, D), 0.25, 1.5, ((0, 128),))
    routes_keys = jax.random.split(jax.random.fold_in(key_list[2], 1), TOKENS // TOK_DEV)
    routes_turns = jax.random.permutation(jax.random.fold_in(key_list[2], 3), TOKENS // TOK_DEV)
    routes = jax.vmap(lambda own, number: routed_block(jax.random.fold_in(key_list[2], 2), own, number, TOK_DEV, EXPERTS, TOP, CAP, 2))(routes_keys, routes_turns).reshape((TOKENS, TOP))
    probs = jnp.clip(0.099609375 + 0.9003906 * jax.random.uniform(key_list[3], (TOKENS, TOP), jnp.float32) ** block_levels(key_list[3], (TOKENS, TOP), ((0, 128),), -0.2, 0.2), 0.099609375, 1.0).astype(jnp.bfloat16)
    w_gate = noise(key_list[4], (EXPERTS, D, FF), D ** -0.5, 0.09375, ((0, 8),))
    w_up = noise(key_list[5], (EXPERTS, D, FF), D ** -0.5, 0.09375, ((0, 8),))
    w_down = noise(key_list[6], (EXPERTS, D, FF), FF ** -0.5, 0.1875, ((0, 8),))
    return dict(tokens=tokens, grad_out=grad_out, routes=routes, probs=probs, w_gate=w_gate, w_up=w_up, w_down=w_down)


def slot_number(routes, experts, capacity):
    flat_routes = routes.reshape(-1)
    onehot = (flat_routes[:, None] == jnp.arange(experts, dtype=jnp.int32)[None, :]).astype(jnp.int32)
    earlier = jnp.cumsum(onehot, axis=0) - onehot
    return flat_routes * capacity + jnp.sum(earlier * onehot, axis=1)


def contract_rows(left_rows, right_rows):
    return lax.dot_general(left_rows, right_rows, (((0,), (0,)), ((), ())), preferred_element_type=jnp.float32)


def expert_rows(row_tokens, row_grads, row_probs, gate_weight, up_weight, down_weight):
    gate_pre = jnp.dot(row_tokens, gate_weight, preferred_element_type=jnp.float32)
    up_pre = jnp.dot(row_tokens, up_weight, preferred_element_type=jnp.float32)
    sigmoid = jax.nn.sigmoid(gate_pre)
    active = gate_pre * sigmoid
    hidden = (active * up_pre).astype(jnp.bfloat16)
    back_grad = jnp.dot(row_grads, down_weight, preferred_element_type=jnp.float32)
    weight_grad = jnp.sum(back_grad * hidden.astype(jnp.float32), axis=1).astype(jnp.bfloat16)
    scaling = row_probs.astype(jnp.float32)[:, None]
    scaled = scaling * back_grad
    grad_gate_pre = (scaled * up_pre * sigmoid * (1.0 + gate_pre * (1.0 - sigmoid))).astype(jnp.bfloat16)
    grad_up_pre = (scaled * active).astype(jnp.bfloat16)
    weighted = (scaling * row_grads.astype(jnp.float32)).astype(jnp.bfloat16)
    contract = (((1,), (1,)), ((), ()))
    row_grad = lax.dot_general(grad_gate_pre, gate_weight, contract, preferred_element_type=jnp.float32)
    row_grad = row_grad + lax.dot_general(grad_up_pre, up_weight, contract, preferred_element_type=jnp.float32)
    return row_grad.astype(jnp.bfloat16), weight_grad, grad_gate_pre, grad_up_pre, hidden, weighted


def reference(tokens, grad_out, routes, probs, w_gate, w_up, w_down):
    blocks = N_DP * N_EXPERT
    pair_count = TOK_DEV * TOP
    total_pairs = TOKENS * TOP
    route_blocks = routes.reshape(blocks, TOK_DEV, TOP)

    def invert(block_routes):
        slot_ids = slot_number(block_routes, EXPERTS, CAP)
        empty_slots = jnp.full((EXPERTS * CAP,), -1, jnp.int32)
        return empty_slots.at[slot_ids].set(jnp.arange(pair_count, dtype=jnp.int32))

    owners = jax.vmap(invert)(route_blocks)
    base_pair = (jnp.arange(blocks, dtype=jnp.int32) * pair_count)[:, None]
    owners = jnp.where(owners >= 0, owners + base_pair, -1)
    owners = owners.reshape(N_DP, N_EXPERT, EXPERTS, CAP).transpose(2, 0, 1, 3).reshape(EXPERTS, N_DP, N_EXPERT * CAP)
    flat_probs = probs.reshape(-1)

    def expert_step(outer, inputs):
        gate_weight, up_weight, down_weight, expert_pairs = inputs

        def group_step(carried, pair_ids):
            pair_grad, pair_weight, gate_total, up_total, down_total = carried
            valid_row = pair_ids >= 0
            safe_pair = jnp.where(valid_row, pair_ids, 0)
            token_row = safe_pair // TOP
            row_tokens = jnp.where(valid_row[:, None], tokens[token_row], jnp.zeros((), tokens.dtype))
            row_grads = jnp.where(valid_row[:, None], grad_out[token_row], jnp.zeros((), grad_out.dtype))
            row_probs = jnp.where(valid_row, flat_probs[safe_pair], jnp.zeros((), probs.dtype))
            row_grad, weight_grad, grad_gate_pre, grad_up_pre, hidden, weighted = expert_rows(
                row_tokens, row_grads, row_probs, gate_weight, up_weight, down_weight)
            part_gate = lax.optimization_barrier(contract_rows(row_tokens, grad_gate_pre).astype(jnp.bfloat16))
            part_up = lax.optimization_barrier(contract_rows(row_tokens, grad_up_pre).astype(jnp.bfloat16))
            part_down = lax.optimization_barrier(contract_rows(weighted, hidden).astype(jnp.bfloat16))
            gate_total = gate_total + part_gate.astype(jnp.float32)
            up_total = up_total + part_up.astype(jnp.float32)
            down_total = down_total + part_down.astype(jnp.float32)
            target = jnp.where(valid_row, pair_ids, total_pairs)
            pair_grad = pair_grad.at[target].set(row_grad, mode="drop")
            pair_weight = pair_weight.at[target].set(weight_grad, mode="drop")
            return (pair_grad, pair_weight, gate_total, up_total, down_total), None

        zero_sum = jnp.zeros((D, FF), jnp.float32)
        start_state = (outer[0], outer[1], zero_sum, zero_sum, zero_sum)
        final_state, _ = lax.scan(group_step, start_state, expert_pairs)
        pair_grad, pair_weight, gate_total, up_total, down_total = final_state
        sums_out = (gate_total.astype(jnp.bfloat16), up_total.astype(jnp.bfloat16), down_total.astype(jnp.bfloat16))
        return (pair_grad, pair_weight), sums_out

    start_outer = (jnp.zeros((total_pairs, D), jnp.bfloat16), jnp.zeros((total_pairs,), jnp.bfloat16))
    final_outer, grads = lax.scan(expert_step, start_outer, (w_gate, w_up, w_down, owners))
    pair_grad, pair_weight = final_outer
    grad_tokens = jnp.sum(pair_grad.reshape(TOKENS, TOP, D).astype(jnp.float32), axis=1).astype(jnp.bfloat16)
    grad_weights = pair_weight.reshape(TOKENS, TOP)
    return grad_tokens, grad_weights, grads[0], grads[1], grads[2]
```

```python
import functools

import jax
import jax.numpy as jnp
from jax import lax
from jax.experimental import pallas as pl
from jax.experimental.pallas import tpu as pltpu
from jax.sharding import PartitionSpec as P

D = 3584
FF = 1024
TOP = 2
CAP = 64
EXPERTS = 8
ROWS = EXPERTS * CAP
TOK = 128
EXTRA = 128
WIDE = D + EXTRA
TILE = 512
NT = D // TILE
NZ = 4
ZB = D // NZ
SUB = ZB // 4
HALF = FF // 2
BF = jnp.bfloat16
F32 = jnp.float32
FIRST = (((0,), (0,)), ((), ()))
LAST = (((1,), (1,)), ((), ()))
MB = 1 << 20


def params(limit=48):
    return pltpu.CompilerParams(vmem_limit_bytes=limit * MB)


def cost(flops, nbytes, trans=0):
    return pl.CostEstimate(flops=flops, bytes_accessed=nbytes, transcendentals=trans)


def place_kernel(routes_ref, tokens_ref, picks_ref, out_ref):
    @pl.when(pl.program_id(0) == 0)
    def _():
        routes = routes_ref[...]
        ids = lax.broadcasted_iota(jnp.int32, (TOK, EXPERTS), 1)
        first = (routes[:, 0:1] == ids).astype(F32).astype(BF)
        second = (routes[:, 1:2] == ids).astype(F32).astype(BF)
        row = lax.broadcasted_iota(jnp.int32, (TOK, TOK), 0)
        col = lax.broadcasted_iota(jnp.int32, (TOK, TOK), 1)
        before = (row < col).astype(F32).astype(BF)
        same = (row == col).astype(F32).astype(BF)
        rank = lax.dot_general(first + second, before, FIRST, preferred_element_type=F32)
        slot = lax.broadcasted_iota(jnp.int32, (CAP, TOK), 0).astype(F32)
        for k, named in enumerate((first, second)):
            named_t = lax.dot_general(named, same, FIRST, preferred_element_type=F32)
            for e in range(EXPERTS):
                hit = (slot == rank[e : e + 1, :]) & (named_t[e : e + 1, :] > 0.5)
                picks_ref[k, e * CAP : (e + 1) * CAP, :] = hit.astype(F32).astype(BF)

    both = picks_ref[0] + picks_ref[1]
    out_ref[...] = jnp.dot(both, tokens_ref[...], preferred_element_type=F32).astype(BF)


def place_tokens(routes, tokens):
    return pl.pallas_call(
        place_kernel,
        grid=(NT,),
        in_specs=[
            pl.BlockSpec((TOK, TOP), lambda i: (0, 0)),
            pl.BlockSpec((TOK, TILE), lambda i: (0, i)),
        ],
        out_specs=[
            pl.BlockSpec((TOP, ROWS, TOK), lambda i: (0, 0, 0)),
            pl.BlockSpec((ROWS, TILE), lambda i: (0, i)),
        ],
        out_shape=[
            jax.ShapeDtypeStruct((TOP, ROWS, TOK), BF),
            jax.ShapeDtypeStruct((ROWS, D), BF),
        ],
        compiler_params=params(),
        cost_estimate=cost(2 * ROWS * TOK * D, 5 * MB),
    )(routes, tokens)


def grads_kernel(picks_ref, probs_ref, grads_ref, out_ref):
    step = pl.program_id(0)

    @pl.when(step < NT)
    def _():
        both = picks_ref[0] + picks_ref[1]
        out_ref[...] = jnp.dot(both, grads_ref[...], preferred_element_type=F32).astype(BF)

    @pl.when(step == NT)
    def _():
        probs = probs_ref[...].astype(F32)
        p0 = jnp.broadcast_to(probs[:, 0:1], (TOK, EXTRA)).astype(BF)
        p1 = jnp.broadcast_to(probs[:, 1:2], (TOK, EXTRA)).astype(BF)
        spread = jnp.dot(picks_ref[0], p0, preferred_element_type=F32)
        spread = spread + jnp.dot(picks_ref[1], p1, preferred_element_type=F32)
        out_ref[:, :EXTRA] = spread.astype(BF)


def place_grads(picks, probs, grads):
    return pl.pallas_call(
        grads_kernel,
        grid=(NT + 1,),
        in_specs=[
            pl.BlockSpec((TOP, ROWS, TOK), lambda i: (0, 0, 0)),
            pl.BlockSpec((TOK, TOP), lambda i: (0, 0)),
            pl.BlockSpec((TOK, TILE), lambda i: (0, jnp.minimum(i, NT - 1))),
        ],
        out_specs=pl.BlockSpec((ROWS, TILE), lambda i: (0, i)),
        out_shape=jax.ShapeDtypeStruct((ROWS, WIDE), BF),
        compiler_params=params(),
        cost_estimate=cost(2 * ROWS * TOK * D, 5 * MB),
    )(picks, probs, grads)


def forward_kernel(x_ref, gate_ref, up_ref, hidden_ref, active_ref, slope_ref):
    x = x_ref[...]
    gate = jnp.dot(x, gate_ref[...], preferred_element_type=F32)
    up = jnp.dot(x, up_ref[...], preferred_element_type=F32)
    s = jax.nn.sigmoid(gate)
    active = gate * s
    hidden_ref[...] = (active * up).astype(BF)
    active_ref[...] = active
    slope_ref[...] = up * s * (1.0 + gate * (1.0 - s))


def forward(x, gate, up):
    n = 256
    return pl.pallas_call(
        forward_kernel,
        grid=(FF // n,),
        in_specs=[
            pl.BlockSpec((ROWS, D), lambda i: (0, 0)),
            pl.BlockSpec((D, n), lambda i: (0, i)),
            pl.BlockSpec((D, n), lambda i: (0, i)),
        ],
        out_specs=[pl.BlockSpec((ROWS, n), lambda i: (0, i))] * 3,
        out_shape=[
            jax.ShapeDtypeStruct((ROWS, FF), BF),
            jax.ShapeDtypeStruct((ROWS, FF), F32),
            jax.ShapeDtypeStruct((ROWS, FF), F32),
        ],
        compiler_params=params(),
        cost_estimate=cost(4 * ROWS * D * FF, 23 * MB, ROWS * FF),
    )(x, gate, up)


def backward_kernel(g_ref, down_ref, hidden_ref, active_ref, slope_ref, gg_ref, gu_ref, wg_ref, total):
    step = pl.program_id(0)
    back = jnp.dot(g_ref[:, :D], down_ref[...], preferred_element_type=F32)
    part = jnp.sum(back * hidden_ref[...].astype(F32), axis=1, keepdims=True)

    @pl.when(step == 0)
    def _():
        total[...] = jnp.zeros_like(total)

    total[...] += jnp.broadcast_to(part, total.shape)
    scaled = g_ref[:, D : D + 1].astype(F32) * back
    gg_ref[...] = (scaled * slope_ref[...]).astype(BF)
    gu_ref[...] = (scaled * active_ref[...]).astype(BF)
    wg_ref[...] = total[...].astype(BF)


def backward(g, down, hidden, active, slope):
    n = 256
    tile = pl.BlockSpec((ROWS, n), lambda i: (0, i))
    return pl.pallas_call(
        backward_kernel,
        grid=(FF // n,),
        in_specs=[
            pl.BlockSpec((ROWS, WIDE), lambda i: (0, 0)),
            pl.BlockSpec((D, n), lambda i: (0, i)),
            tile,
            tile,
            tile,
        ],
        out_specs=[tile, tile, pl.BlockSpec((ROWS, EXTRA), lambda i: (0, 0))],
        out_shape=[
            jax.ShapeDtypeStruct((ROWS, FF), BF),
            jax.ShapeDtypeStruct((ROWS, FF), BF),
            jax.ShapeDtypeStruct((ROWS, EXTRA), BF),
        ],
        scratch_shapes=[pltpu.VMEM((ROWS, EXTRA), F32)],
        compiler_params=params(),
        cost_estimate=cost(2 * ROWS * D * FF, 18 * MB),
    )(g, down, hidden, active, slope)


def rows_kernel(gg_ref, gu_ref, gate_ref, up_ref, wg_ref, out_ref):
    step = pl.program_id(0)

    @pl.when(step < NT)
    def _():
        grad = lax.dot_general(gg_ref[...], gate_ref[...], LAST, preferred_element_type=F32)
        grad = grad + lax.dot_general(gu_ref[...], up_ref[...], LAST, preferred_element_type=F32)
        out_ref[...] = grad.astype(BF)

    @pl.when(step == NT)
    def _():
        out_ref[:, :EXTRA] = wg_ref[...]


def row_grads(gg, gu, gate, up, wg):
    clamp = lambda i: (jnp.minimum(i, NT - 1), 0)
    return pl.pallas_call(
        rows_kernel,
        grid=(NT + 1,),
        in_specs=[
            pl.BlockSpec((ROWS, FF), lambda i: (0, 0)),
            pl.BlockSpec((ROWS, FF), lambda i: (0, 0)),
            pl.BlockSpec((TILE, FF), clamp),
            pl.BlockSpec((TILE, FF), clamp),
            pl.BlockSpec((ROWS, EXTRA), lambda i: (0, 0)),
        ],
        out_specs=pl.BlockSpec((ROWS, TILE), lambda i: (0, i)),
        out_shape=jax.ShapeDtypeStruct((ROWS, WIDE), BF),
        compiler_params=params(),
        cost_estimate=cost(4 * ROWS * D * FF, 21 * MB),
    )(gg, gu, gate, up, wg)


def partial_kernel(scaled, place_ref, x_ref, p_ref, h_ref, send_ref, keep_ref):
    x = x_ref[...]
    if scaled:
        x = (p_ref[:, 0:1].astype(F32) * x.astype(F32)).astype(BF)
    part = lax.dot_general(x, h_ref[...], FIRST, preferred_element_type=F32).astype(BF)
    odd = place_ref[2] == 1
    for j in range(2):
        even_rows = part[2 * j * SUB : (2 * j + 1) * SUB]
        odd_rows = part[(2 * j + 1) * SUB : (2 * j + 2) * SUB]
        rows = slice(j * SUB, (j + 1) * SUB)
        send_ref[0, rows, :] = jnp.where(odd, even_rows, odd_rows)
        keep_ref[0, rows, :] = jnp.where(odd, odd_rows, even_rows)


def partial(place, x, p, h, scaled):
    last = (p.shape[1] // EXTRA) - 1
    return pl.pallas_call(
        functools.partial(partial_kernel, scaled),
        grid_spec=pltpu.PrefetchScalarGridSpec(
            num_scalar_prefetch=1,
            grid=(2,),
            in_specs=[
                pl.BlockSpec((ROWS, ZB), lambda i, place: (0, place[i])),
                pl.BlockSpec((ROWS, EXTRA), lambda i, place: (0, last)),
                pl.BlockSpec((ROWS, HALF), lambda i, place: (0, i)),
            ],
            out_specs=[pl.BlockSpec((1, 2 * SUB, HALF), lambda i, place: (i, 0, 0))] * 2,
        ),
        out_shape=[jax.ShapeDtypeStruct((2, 2 * SUB, HALF), BF)] * 2,
        compiler_params=params(),
        cost_estimate=cost(2 * ROWS * ZB * FF, 5 * MB),
    )(place, x, p, h)


def combine_kernel(picks_ref, rows_ref, tokens_ref, weights_ref):
    step = pl.program_id(0)

    @pl.when(step < NT)
    def _():
        both = picks_ref[0] + picks_ref[1]
        tokens_ref[...] = lax.dot_general(
            both, rows_ref[...], FIRST, preferred_element_type=F32
        ).astype(BF)

    @pl.when(step == NT)
    def _():
        found = [
            lax.dot_general(
                picks_ref[k], rows_ref[:, :EXTRA], FIRST, preferred_element_type=F32
            )
            for k in range(TOP)
        ]
        lane = lax.broadcasted_iota(jnp.int32, (TOK, EXTRA), 1)
        weights_ref[...] = jnp.where(lane == 0, found[0], found[1]).astype(BF)[:, :TOP]


def combine(picks, rows):
    return pl.pallas_call(
        combine_kernel,
        grid=(NT + 1,),
        in_specs=[
            pl.BlockSpec((TOP, ROWS, TOK), lambda i: (0, 0, 0)),
            pl.BlockSpec((ROWS, TILE), lambda i: (0, i)),
        ],
        out_specs=[
            pl.BlockSpec((TOK, TILE), lambda i: (0, jnp.minimum(i, NT - 1))),
            pl.BlockSpec((TOK, TOP), lambda i: (0, 0)),
        ],
        out_shape=[
            jax.ShapeDtypeStruct((TOK, D), BF),
            jax.ShapeDtypeStruct((TOK, TOP), BF),
        ],
        compiler_params=params(),
        cost_estimate=cost(2 * ROWS * TOK * D, 5 * MB),
    )(picks, rows)


def moves(f):
    pairs = []
    for z in range(NZ):
        for x in range(2):
            for c in range(2):
                tz, tx, tc = f(z, x, c)
                pairs.append((z * 4 + x * 2 + c, (tz % NZ) * 4 + tx * 2 + tc))
    return pairs


TO_CORE = moves(lambda z, x, c: (z, x, 1 - c))
TO_UP = moves(lambda z, x, c: (z + 1, x, c))
TO_DOWN = moves(lambda z, x, c: (z - 1, x, c))
TO_X = moves(lambda z, x, c: (z, 1 - x, c))


def add(*parts):
    total = parts[0].astype(F32)
    for part in parts[1:]:
        total = total + part.astype(F32)
    return total.astype(BF)


def summed(z, x, c, left, p, right, scaled):
    up = down = None
    for step in range(NZ):
        place = jnp.stack([(z - 1 - step) % NZ, (z + 1 + step) % NZ, c]).astype(jnp.int32)
        send, keep = partial(place, left, p, right, scaled)
        other = lax.ppermute(send, "dp", TO_CORE)
        if step == 0:
            up, down = add(keep[0], other[0]), add(keep[1], other[1])
        else:
            up, down = add(keep[0], other[0], up), add(keep[1], other[1], down)
        if step < NZ - 1:
            up = lax.ppermute(up, "dp", TO_UP)
            down = lax.ppermute(down, "dp", TO_DOWN)
    full = jnp.concatenate([up.reshape(2, SUB, HALF), down.reshape(2, SUB, HALF)], axis=2)
    mine = jnp.where(x == 0, full[0], full[1])
    away = lax.ppermute(jnp.where(x == 0, full[1], full[0]), "dp", TO_X)
    return add(mine, away)[None]


def exchange(rows):
    width = rows.shape[1]
    out = lax.all_to_all(
        rows.reshape(EXPERTS, CAP, width), "expert", split_axis=0, concat_axis=0, tiled=True
    )
    return out.reshape(ROWS, width)


def local(tokens, grad_out, routes, probs, w_gate, w_up, w_down):
    where = lax.axis_index("dp")
    z, x, c = where // 4, (where // 2) % 2, where % 2
    gate, up, down = w_gate[0], w_up[0], w_down[0]
    picks, send_tokens = place_tokens(routes, tokens)
    row_tokens = exchange(send_tokens)
    send_grads = place_grads(picks, probs, grad_out)
    row_grads_in = exchange(send_grads)
    hidden, active, slope = forward(row_tokens, gate, up)
    gg, gu, wg = backward(row_grads_in, down, hidden, active, slope)
    grad_down = summed(z, x, c, row_grads_in, row_grads_in, hidden, True)
    grad_gate = summed(z, x, c, row_tokens, row_grads_in, gg, False)
    grad_up = summed(z, x, c, row_tokens, row_grads_in, gu, False)
    returned = exchange(row_grads(gg, gu, gate, up, wg))
    grad_tokens, grad_weights = combine(picks, returned)
    return (grad_tokens, grad_weights, grad_gate, grad_up, grad_down)


def solution(mesh):
    spec = P(("dp", "expert"), None)
    weight = P("expert", None, None)
    out = P("expert", "dp", None)
    return jax.shard_map(
        local,
        mesh=mesh,
        in_specs=(spec, spec, spec, spec, weight, weight, weight),
        out_specs=(spec, spec, out, out, out),
        check_vma=False,
    )
```

```python
import functools

import jax
import jax.numpy as jnp
import numpy as np
from jax import lax
from jax.experimental import pallas as pl
from jax.experimental.pallas import tpu as pltpu
from jax.sharding import PartitionSpec as P

D = 3584
FF = 1024
TOP = 2
CAP = 64
EXPERTS = 8
ROWS = EXPERTS * CAP
TOK = 128
EXTRA = 128
WIDE = D + EXTRA
TILE = 512
NT = D // TILE
NZ = 4
ZB = D // NZ
SUB = ZB // 4
HALF = FF // 2
BF = jnp.bfloat16
F32 = jnp.float32
FIRST = (((0,), (0,)), ((), ()))
LAST = (((1,), (1,)), ((), ()))
MB = 1 << 20


def params(limit=60):
    return pltpu.CompilerParams(vmem_limit_bytes=limit * MB)


def cost(flops, nbytes, trans=0):
    return pl.CostEstimate(flops=flops, bytes_accessed=nbytes, transcendentals=trans)


def place_kernel(routes_ref, tokens_ref, picks_ref, out_ref):
    @pl.when(pl.program_id(0) == 0)
    def _():
        routes = routes_ref[...]
        ids = lax.broadcasted_iota(jnp.int32, (TOK, EXPERTS), 1)
        first = (routes[:, 0:1] == ids).astype(F32).astype(BF)
        second = (routes[:, 1:2] == ids).astype(F32).astype(BF)
        row = lax.broadcasted_iota(jnp.int32, (TOK, TOK), 0)
        col = lax.broadcasted_iota(jnp.int32, (TOK, TOK), 1)
        before = (row < col).astype(F32).astype(BF)
        same = (row == col).astype(F32).astype(BF)
        rank = lax.dot_general(first + second, before, FIRST, preferred_element_type=F32)
        slot = lax.broadcasted_iota(jnp.int32, (CAP, TOK), 0).astype(F32)
        for k, named in enumerate((first, second)):
            named_t = lax.dot_general(named, same, FIRST, preferred_element_type=F32)
            for e in range(EXPERTS):
                hit = (slot == rank[e : e + 1, :]) & (named_t[e : e + 1, :] > 0.5)
                picks_ref[k, e * CAP : (e + 1) * CAP, :] = hit.astype(F32).astype(BF)

    both = picks_ref[0] + picks_ref[1]
    out_ref[...] = jnp.dot(both, tokens_ref[...], preferred_element_type=F32).astype(BF)


def place_tokens(routes, tokens):
    return pl.pallas_call(
        place_kernel,
        grid=(NT,),
        in_specs=[
            pl.BlockSpec((TOK, TOP), lambda i: (0, 0)),
            pl.BlockSpec((TOK, TILE), lambda i: (0, i)),
        ],
        out_specs=[
            pl.BlockSpec((TOP, ROWS, TOK), lambda i: (0, 0, 0)),
            pl.BlockSpec((ROWS, TILE), lambda i: (0, i)),
        ],
        out_shape=[
            jax.ShapeDtypeStruct((TOP, ROWS, TOK), BF),
            jax.ShapeDtypeStruct((ROWS, D), BF),
        ],
        compiler_params=params(),
        cost_estimate=cost(2 * ROWS * TOK * D, 5 * MB),
    )(routes, tokens)


def grads_kernel(picks_ref, probs_ref, grads_ref, out_ref):
    step = pl.program_id(0)

    @pl.when(step < NT)
    def _():
        both = picks_ref[0] + picks_ref[1]
        out_ref[...] = jnp.dot(both, grads_ref[...], preferred_element_type=F32).astype(BF)

    @pl.when(step == NT)
    def _():
        probs = probs_ref[...].astype(F32)
        p0 = jnp.broadcast_to(probs[:, 0:1], (TOK, EXTRA)).astype(BF)
        p1 = jnp.broadcast_to(probs[:, 1:2], (TOK, EXTRA)).astype(BF)
        spread = jnp.dot(picks_ref[0], p0, preferred_element_type=F32)
        spread = spread + jnp.dot(picks_ref[1], p1, preferred_element_type=F32)
        out_ref[:, :EXTRA] = spread.astype(BF)


def place_grads(picks, probs, grads):
    return pl.pallas_call(
        grads_kernel,
        grid=(NT + 1,),
        in_specs=[
            pl.BlockSpec((TOP, ROWS, TOK), lambda i: (0, 0, 0)),
            pl.BlockSpec((TOK, TOP), lambda i: (0, 0)),
            pl.BlockSpec((TOK, TILE), lambda i: (0, jnp.minimum(i, NT - 1))),
        ],
        out_specs=pl.BlockSpec((ROWS, TILE), lambda i: (0, i)),
        out_shape=jax.ShapeDtypeStruct((ROWS, WIDE), BF),
        compiler_params=params(),
        cost_estimate=cost(2 * ROWS * TOK * D, 5 * MB),
    )(picks, probs, grads)


def forward_kernel(x_ref, gate_ref, up_ref, hidden_ref, active_ref, slope_ref):
    x = x_ref[...]
    gate = jnp.dot(x, gate_ref[...], preferred_element_type=F32)
    up = jnp.dot(x, up_ref[...], preferred_element_type=F32)
    s = jax.nn.sigmoid(gate)
    active = gate * s
    hidden_ref[...] = (active * up).astype(BF)
    active_ref[...] = active
    slope_ref[...] = up * s * (1.0 + gate * (1.0 - s))


def forward(x, gate, up):
    n = 256
    return pl.pallas_call(
        forward_kernel,
        grid=(FF // n,),
        in_specs=[
            pl.BlockSpec((ROWS, D), lambda i: (0, 0)),
            pl.BlockSpec((D, n), lambda i: (0, i)),
            pl.BlockSpec((D, n), lambda i: (0, i)),
        ],
        out_specs=[pl.BlockSpec((ROWS, n), lambda i: (0, i))] * 3,
        out_shape=[
            jax.ShapeDtypeStruct((ROWS, FF), BF),
            jax.ShapeDtypeStruct((ROWS, FF), F32),
            jax.ShapeDtypeStruct((ROWS, FF), F32),
        ],
        compiler_params=params(),
        cost_estimate=cost(4 * ROWS * D * FF, 23 * MB, ROWS * FF),
    )(x, gate, up)


def backward_kernel(g_ref, down_ref, hidden_ref, active_ref, slope_ref, *refs):
    both_ref, wg_ref, total = refs[-3:]
    step = pl.program_id(0)
    back = jnp.dot(g_ref[:, :D], down_ref[...], preferred_element_type=F32)
    part = jnp.sum(back * hidden_ref[...].astype(F32), axis=1, keepdims=True)

    @pl.when(step == 0)
    def _():
        total[...] = jnp.zeros_like(total)

    total[...] += jnp.broadcast_to(part, total.shape)
    scaled = g_ref[:, D : D + 1].astype(F32) * back
    both_ref[0] = (scaled * slope_ref[...]).astype(BF)
    both_ref[1] = (scaled * active_ref[...]).astype(BF)
    wg_ref[...] = total[...].astype(BF)


def backward(g, down, hidden, active, slope, after=()):
    n = 256
    tile = pl.BlockSpec((ROWS, n), lambda i: (0, i))
    return pl.pallas_call(
        backward_kernel,
        grid=(FF // n,),
        in_specs=[
            pl.BlockSpec((ROWS, WIDE), lambda i: (0, 0)),
            pl.BlockSpec((D, n), lambda i: (0, i)),
            tile,
            tile,
            tile,
        ]
        + [pl.BlockSpec(memory_space=pl.ANY)] * len(after),
        out_specs=[
            pl.BlockSpec((2, ROWS, n), lambda i: (0, 0, i)),
            pl.BlockSpec((ROWS, EXTRA), lambda i: (0, 0)),
        ],
        out_shape=[
            jax.ShapeDtypeStruct((2, ROWS, FF), BF),
            jax.ShapeDtypeStruct((ROWS, EXTRA), BF),
        ],
        scratch_shapes=[pltpu.VMEM((ROWS, EXTRA), F32)],
        compiler_params=params(),
        cost_estimate=cost(2 * ROWS * D * FF, 18 * MB),
    )(g, down, hidden, active, slope, *after)


def rows_kernel(both_ref, gate_ref, up_ref, wg_ref, *refs):
    out_ref = refs[-1]
    step = pl.program_id(0)

    @pl.when(step < NT)
    def _():
        grad = lax.dot_general(both_ref[0], gate_ref[...], LAST, preferred_element_type=F32)
        grad = grad + lax.dot_general(both_ref[1], up_ref[...], LAST, preferred_element_type=F32)
        out_ref[...] = grad.astype(BF)

    @pl.when(step == NT)
    def _():
        out_ref[:, :EXTRA] = wg_ref[...]


def row_grads(both, gate, up, wg, after=()):
    clamp = lambda i: (jnp.minimum(i, NT - 1), 0)
    return pl.pallas_call(
        rows_kernel,
        grid=(NT + 1,),
        in_specs=[
            pl.BlockSpec((2, ROWS, FF), lambda i: (0, 0, 0)),
            pl.BlockSpec((TILE, FF), clamp),
            pl.BlockSpec((TILE, FF), clamp),
            pl.BlockSpec((ROWS, EXTRA), lambda i: (0, 0)),
        ]
        + [pl.BlockSpec(memory_space=pl.ANY)] * len(after),
        out_specs=pl.BlockSpec((ROWS, TILE), lambda i: (0, i)),
        out_shape=jax.ShapeDtypeStruct((ROWS, WIDE), BF),
        compiler_params=params(),
        cost_estimate=cost(4 * ROWS * D * FF, 21 * MB),
    )(both, gate, up, wg, *after)


def turned_kernel(scaled, deps, place_ref, x_ref, p_ref, *refs):
    send_ref, keep_ref, turned = refs[deps:]
    x = x_ref[...]
    if scaled:
        x = (p_ref[:, 0:1].astype(F32) * x.astype(F32)).astype(BF)
    turned[...] = x.T
    core = place_ref[8]
    for j in range(2):
        rows = slice(j * SUB, (j + 1) * SUB)
        far = pl.multiple_of((2 * j + 1 - core) * SUB, SUB)
        near = pl.multiple_of((2 * j + core) * SUB, SUB)
        send_ref[0, rows, :] = turned[pl.ds(far, SUB), :]
        keep_ref[0, rows, :] = turned[pl.ds(near, SUB), :]


def turned(place, x, p, scaled, after=()):
    last = (p.shape[1] // EXTRA) - 1
    send, keep = pl.pallas_call(
        functools.partial(turned_kernel, scaled, len(after)),
        grid_spec=pltpu.PrefetchScalarGridSpec(
            num_scalar_prefetch=1,
            grid=(NZ,),
            in_specs=[
                pl.BlockSpec((ROWS, ZB), lambda i, place: (0, i)),
                pl.BlockSpec((ROWS, EXTRA), lambda i, place: (0, last)),
            ]
            + [pl.BlockSpec(memory_space=pl.ANY)] * len(after),
            out_specs=[pl.BlockSpec((1, 2 * SUB, ROWS), lambda i, place: (i, 0, 0))] * 2,
            scratch_shapes=[pltpu.VMEM((ZB, ROWS), BF)],
        ),
        out_shape=[jax.ShapeDtypeStruct((NZ, 2 * SUB, ROWS), BF)] * 2,
        compiler_params=params(),
        cost_estimate=cost(ROWS * D, 8 * MB),
    )(place, x, p, *after)
    return keep, lax.ppermute(send, "dp", TO_CORE)


def combine_kernel(picks_ref, rows_ref, *refs):
    tokens_ref, weights_ref = refs[-2:]
    step = pl.program_id(0)

    @pl.when(step < NT)
    def _():
        both = picks_ref[0] + picks_ref[1]
        tokens_ref[...] = lax.dot_general(
            both, rows_ref[...], FIRST, preferred_element_type=F32
        ).astype(BF)

    @pl.when(step == NT)
    def _():
        found = [
            lax.dot_general(
                picks_ref[k], rows_ref[:, :EXTRA], FIRST, preferred_element_type=F32
            )
            for k in range(TOP)
        ]
        lane = lax.broadcasted_iota(jnp.int32, (TOK, EXTRA), 1)
        weights_ref[...] = jnp.where(lane == 0, found[0], found[1]).astype(BF)[:, :TOP]


def combine(picks, rows, after=()):
    return pl.pallas_call(
        combine_kernel,
        grid=(NT + 1,),
        in_specs=[
            pl.BlockSpec((TOP, ROWS, TOK), lambda i: (0, 0, 0)),
            pl.BlockSpec((ROWS, TILE), lambda i: (0, i)),
        ]
        + [pl.BlockSpec(memory_space=pl.ANY)] * len(after),
        out_specs=[
            pl.BlockSpec((TOK, TILE), lambda i: (0, jnp.minimum(i, NT - 1))),
            pl.BlockSpec((TOK, TOP), lambda i: (0, 0)),
        ],
        out_shape=[
            jax.ShapeDtypeStruct((TOK, D), BF),
            jax.ShapeDtypeStruct((TOK, TOP), BF),
        ],
        compiler_params=params(),
        cost_estimate=cost(2 * ROWS * TOK * D, 5 * MB),
    )(picks, rows, *after)


def moves(f):
    pairs = []
    for z in range(NZ):
        for x in range(2):
            for c in range(2):
                tz, tx, tc = f(z, x, c)
                pairs.append((z * 4 + x * 2 + c, (tz % NZ) * 4 + tx * 2 + tc))
    return pairs


TO_CORE = moves(lambda z, x, c: (z, x, 1 - c))
TO_UP = moves(lambda z, x, c: (z + 1, x, c))
TO_DOWN = moves(lambda z, x, c: (z - 1, x, c))
TO_X = moves(lambda z, x, c: (z, 1 - x, c))


def add(*parts):
    total = parts[0].astype(F32)
    for part in parts[1:]:
        total = total + part.astype(F32)
    return total.astype(BF)


def step_kernel(moved, last, place_ref, left_a, left_b, right_a, right_b, *refs):
    way = pl.program_id(0) // 2
    rights = [r[0] if len(r.shape) == 3 else r[...] for r in (right_a, right_b)]
    total = jnp.dot(left_a[0], rights[0], preferred_element_type=F32)
    total = total + jnp.dot(left_b[0], rights[1], preferred_element_type=F32)
    if last:
        mine_ref, away_ref, full = refs[-3:]
        for k in range(2):

            @pl.when(way == k)
            def _():
                full[...] = (total + refs[k][...].astype(F32)).astype(BF)

        x = place_ref[9]
        mine_ref[0] = full[pl.ds(pl.multiple_of(x * SUB, SUB), SUB), :]
        away_ref[0] = full[pl.ds(pl.multiple_of((1 - x) * SUB, SUB), SUB), :]
    else:
        for k, out_ref in enumerate(refs[-2:]):

            @pl.when(way == k)
            def _():
                out_ref[...] = (total + refs[k][...].astype(F32) if moved else total).astype(BF)


def ring_step(place, step, lefts, rights, moved=(), after=()):
    if rights[0].ndim == 3:
        width = rights[0].shape[2]
        n = width // 2
        right = pl.BlockSpec((1, ROWS, n), lambda i, place: (i // 2, 0, i % 2))
    else:
        width = rights[0].shape[1] // 2
        n = width // 2
        right = pl.BlockSpec((ROWS, n), lambda i, place: (0, i))
    left = pl.BlockSpec((1, 2 * SUB, ROWS), lambda i, place: (place[2 * step + i // 2], 0, 0))
    up = pl.BlockSpec((2 * SUB, n), lambda i, place: (0, jnp.minimum(i, 1)))
    down = pl.BlockSpec((2 * SUB, n), lambda i, place: (0, jnp.maximum(i - 2, 0)))
    last = step == NZ - 1
    if last:
        out_specs = [pl.BlockSpec((1, SUB, n), lambda i, place: (i // 2, 0, i % 2))] * 2
        out_shape = [jax.ShapeDtypeStruct((2, SUB, width), BF)] * 2
        scratch = [pltpu.VMEM((2 * SUB, n), BF)]
    else:
        out_specs = [up, down]
        out_shape = [jax.ShapeDtypeStruct((2 * SUB, width), BF)] * 2
        scratch = []
    first, second = pl.pallas_call(
        functools.partial(step_kernel, len(moved) > 0, last),
        grid_spec=pltpu.PrefetchScalarGridSpec(
            num_scalar_prefetch=1,
            grid=(4,),
            in_specs=[left, left, right, right]
            + [up, down][: len(moved)]
            + [pl.BlockSpec(memory_space=pl.ANY)] * len(after),
            out_specs=out_specs,
            scratch_shapes=scratch,
        ),
        out_shape=out_shape,
        compiler_params=params(),
        cost_estimate=cost(1 if width == FF else 40_000_000_000, 1),
    )(place, *lefts, *rights, *moved, *after)
    if last:
        return first, lax.ppermute(second, "dp", TO_X)
    return lax.ppermute(first, "dp", TO_UP), lax.ppermute(second, "dp", TO_DOWN), first


PLACES = np.array(
    [
        [v for s in range(NZ) for v in ((z - 1 - s) % NZ, (z + 1 + s) % NZ)] + [c, x]
        for z in range(NZ)
        for x in range(2)
        for c in range(2)
    ],
    np.int32,
)


def exchange(rows):
    width = rows.shape[1]
    out = lax.all_to_all(
        rows.reshape(EXPERTS, CAP, width), "expert", split_axis=0, concat_axis=0, tiled=True
    )
    return out.reshape(ROWS, width)


def local(tokens, grad_out, routes, probs, w_gate, w_up, w_down):
    place = lax.dynamic_index_in_dim(jnp.asarray(PLACES), lax.axis_index("dp"), 0, keepdims=False)
    gate, up, down = w_gate[0], w_up[0], w_down[0]
    picks, send_tokens = place_tokens(routes, tokens)
    row_tokens = exchange(send_tokens)
    send_grads = place_grads(picks, probs, grad_out)
    row_grads_in = exchange(send_grads)
    hidden, active, slope = forward(row_tokens, gate, up)
    lefts = turned(place, row_tokens, row_tokens, False, after=(hidden,))
    hiddens = (hidden, lax.ppermute(hidden, "dp", TO_CORE))
    both, wg = backward(
        row_grads_in, down, hidden, active, slope, after=(lefts[0], lefts[1], hiddens[1])
    )
    boths = (both, lax.ppermute(both, "dp", TO_CORE))
    dlefts = turned(place, row_grads_in, row_grads_in, True, after=(both,))
    *moved, done = ring_step(place, 0, lefts, boths, after=dlefts[:1])
    *dmoved, done = ring_step(place, 0, dlefts, hiddens, after=(done,))
    sent_rows = row_grads(both, gate, up, wg, after=(done,))
    returned = exchange(sent_rows)
    *moved, done = ring_step(place, 1, lefts, boths, moved, after=(sent_rows,))
    *dmoved, done = ring_step(place, 1, dlefts, hiddens, dmoved, after=(done,))
    *moved, done = ring_step(place, 2, lefts, boths, moved, after=(done,))
    *dmoved, done = ring_step(place, 2, dlefts, hiddens, dmoved, after=(done,))
    mine, away = ring_step(place, 3, lefts, boths, moved, after=(done,))
    grad_tokens, grad_weights = combine(picks, returned, after=(mine,))
    dmine, daway = ring_step(place, 3, dlefts, hiddens, dmoved, after=(grad_tokens,))
    grad_gate = add(mine[0], away[0])[None]
    grad_up = add(mine[1], away[1])[None]
    grad_down = jnp.concatenate([add(dmine[0], daway[0]), add(dmine[1], daway[1])], axis=1)[None]
    return (grad_tokens, grad_weights, grad_gate, grad_up, grad_down)


def solution(mesh):
    spec = P(("dp", "expert"), None)
    weight = P("expert", None, None)
    out = P("expert", "dp", None)
    return jax.shard_map(
        local,
        mesh=mesh,
        in_specs=(spec, spec, spec, spec, weight, weight, weight),
        out_specs=(spec, spec, out, out, out),
        check_vma=False,
    )
```

```python
import functools

import jax
import jax.numpy as jnp
import numpy as np
from jax import lax
from jax.experimental import pallas as pl
from jax.experimental.pallas import tpu as pltpu
from jax.sharding import PartitionSpec as P

D = 3584
FF = 1024
TOP = 2
CAP = 64
EXPERTS = 8
ROWS = EXPERTS * CAP
TOK = 128
EXTRA = 128
WIDE = D + EXTRA
TILE = 1792
NT = D // TILE
NZ = 4
ZB = D // NZ
SUB = ZB // 4
HALF = FF // 2
BF = jnp.bfloat16
F32 = jnp.float32
FIRST = (((0,), (0,)), ((), ()))
LAST = (((1,), (1,)), ((), ()))
MB = 1 << 20


def params(limit=60):
    return pltpu.CompilerParams(vmem_limit_bytes=limit * MB)


def cost(flops, nbytes, trans=0):
    return pl.CostEstimate(flops=flops, bytes_accessed=nbytes, transcendentals=trans)


def place_kernel(routes_ref, tokens_ref, picks_ref, out_ref):
    @pl.when(pl.program_id(0) == 0)
    def _():
        routes = routes_ref[...]
        ids = lax.broadcasted_iota(jnp.int32, (TOK, EXPERTS), 1)
        first = (routes[:, 0:1] == ids).astype(F32).astype(BF)
        second = (routes[:, 1:2] == ids).astype(F32).astype(BF)
        row = lax.broadcasted_iota(jnp.int32, (TOK, TOK), 0)
        col = lax.broadcasted_iota(jnp.int32, (TOK, TOK), 1)
        before = (row < col).astype(F32).astype(BF)
        same = (row == col).astype(F32).astype(BF)
        rank = lax.dot_general(first + second, before, FIRST, preferred_element_type=F32)
        slot = lax.broadcasted_iota(jnp.int32, (CAP, TOK), 0).astype(F32)
        for k, named in enumerate((first, second)):
            named_t = lax.dot_general(named, same, FIRST, preferred_element_type=F32)
            for e in range(EXPERTS):
                hit = (slot == rank[e : e + 1, :]) & (named_t[e : e + 1, :] > 0.5)
                picks_ref[k, e * CAP : (e + 1) * CAP, :] = hit.astype(F32).astype(BF)

    both = picks_ref[0] + picks_ref[1]
    out_ref[...] = jnp.dot(both, tokens_ref[...], preferred_element_type=F32).astype(BF)


def place_tokens(routes, tokens):
    return pl.pallas_call(
        place_kernel,
        grid=(NT,),
        in_specs=[
            pl.BlockSpec((TOK, TOP), lambda i: (0, 0)),
            pl.BlockSpec((TOK, TILE), lambda i: (0, i)),
        ],
        out_specs=[
            pl.BlockSpec((TOP, ROWS, TOK), lambda i: (0, 0, 0)),
            pl.BlockSpec((ROWS, TILE), lambda i: (0, i)),
        ],
        out_shape=[
            jax.ShapeDtypeStruct((TOP, ROWS, TOK), BF),
            jax.ShapeDtypeStruct((ROWS, D), BF),
        ],
        compiler_params=params(),
        cost_estimate=cost(2 * ROWS * TOK * D, 5 * MB),
    )(routes, tokens)


def grads_kernel(picks_ref, probs_ref, grads_ref, out_ref):
    step = pl.program_id(0)

    @pl.when(step < NT)
    def _():
        both = picks_ref[0] + picks_ref[1]
        out_ref[...] = jnp.dot(both, grads_ref[...], preferred_element_type=F32).astype(BF)

    @pl.when(step == NT)
    def _():
        probs = probs_ref[...].astype(F32)
        p0 = jnp.broadcast_to(probs[:, 0:1], (TOK, EXTRA)).astype(BF)
        p1 = jnp.broadcast_to(probs[:, 1:2], (TOK, EXTRA)).astype(BF)
        spread = jnp.dot(picks_ref[0], p0, preferred_element_type=F32)
        spread = spread + jnp.dot(picks_ref[1], p1, preferred_element_type=F32)
        out_ref[:, :EXTRA] = spread.astype(BF)


def place_grads(picks, probs, grads):
    return pl.pallas_call(
        grads_kernel,
        grid=(NT + 1,),
        in_specs=[
            pl.BlockSpec((TOP, ROWS, TOK), lambda i: (0, 0, 0)),
            pl.BlockSpec((TOK, TOP), lambda i: (0, 0)),
            pl.BlockSpec((TOK, TILE), lambda i: (0, jnp.minimum(i, NT - 1))),
        ],
        out_specs=pl.BlockSpec((ROWS, TILE), lambda i: (0, i)),
        out_shape=jax.ShapeDtypeStruct((ROWS, WIDE), BF),
        compiler_params=params(),
        cost_estimate=cost(2 * ROWS * TOK * D, 5 * MB),
    )(picks, probs, grads)


def forward_kernel(x_ref, gate_ref, up_ref, hidden_ref, active_ref, slope_ref):
    x = x_ref[...]
    gate = jnp.dot(x, gate_ref[...], preferred_element_type=F32)
    up = jnp.dot(x, up_ref[...], preferred_element_type=F32)
    s = jax.nn.sigmoid(gate)
    active = gate * s
    hidden_ref[...] = (active * up).astype(BF)
    active_ref[...] = active
    slope_ref[...] = up * s * (1.0 + gate * (1.0 - s))


def forward(x, gate, up):
    n = 256
    return pl.pallas_call(
        forward_kernel,
        grid=(FF // n,),
        in_specs=[
            pl.BlockSpec((ROWS, D), lambda i: (0, 0)),
            pl.BlockSpec((D, n), lambda i: (0, i)),
            pl.BlockSpec((D, n), lambda i: (0, i)),
        ],
        out_specs=[pl.BlockSpec((ROWS, n), lambda i: (0, i))] * 3,
        out_shape=[
            jax.ShapeDtypeStruct((ROWS, FF), BF),
            jax.ShapeDtypeStruct((ROWS, FF), F32),
            jax.ShapeDtypeStruct((ROWS, FF), F32),
        ],
        compiler_params=params(),
        cost_estimate=cost(4 * ROWS * D * FF, 23 * MB, ROWS * FF),
    )(x, gate, up)


def backward_kernel(g_ref, down_ref, hidden_ref, active_ref, slope_ref, *refs):
    both_ref, wg_ref, total = refs[-3:]
    step = pl.program_id(0)
    back = jnp.dot(g_ref[:, :D], down_ref[...], preferred_element_type=F32)
    part = jnp.sum(back * hidden_ref[...].astype(F32), axis=1, keepdims=True)

    @pl.when(step == 0)
    def _():
        total[...] = jnp.zeros_like(total)

    total[...] += jnp.broadcast_to(part, total.shape)
    scaled = g_ref[:, D : D + 1].astype(F32) * back
    both_ref[0] = (scaled * slope_ref[...]).astype(BF)
    both_ref[1] = (scaled * active_ref[...]).astype(BF)
    wg_ref[...] = total[...].astype(BF)


def backward(g, down, hidden, active, slope, after=()):
    n = 512
    tile = pl.BlockSpec((ROWS, n), lambda i: (0, i))
    return pl.pallas_call(
        backward_kernel,
        grid=(FF // n,),
        in_specs=[
            pl.BlockSpec((ROWS, WIDE), lambda i: (0, 0)),
            pl.BlockSpec((D, n), lambda i: (0, i)),
            tile,
            tile,
            tile,
        ]
        + [pl.BlockSpec(memory_space=pl.ANY)] * len(after),
        out_specs=[
            pl.BlockSpec((2, ROWS, n), lambda i: (0, 0, i)),
            pl.BlockSpec((ROWS, EXTRA), lambda i: (0, 0)),
        ],
        out_shape=[
            jax.ShapeDtypeStruct((2, ROWS, FF), BF),
            jax.ShapeDtypeStruct((ROWS, EXTRA), BF),
        ],
        scratch_shapes=[pltpu.VMEM((ROWS, EXTRA), F32)],
        compiler_params=params(),
        cost_estimate=cost(2 * ROWS * D * FF, 18 * MB),
    )(g, down, hidden, active, slope, *after)


def rows_kernel(both_ref, gate_ref, up_ref, wg_ref, *refs):
    out_ref = refs[-1]
    step = pl.program_id(0)

    @pl.when(step < NT)
    def _():
        grad = lax.dot_general(both_ref[0], gate_ref[...], LAST, preferred_element_type=F32)
        grad = grad + lax.dot_general(both_ref[1], up_ref[...], LAST, preferred_element_type=F32)
        out_ref[...] = grad.astype(BF)

    @pl.when(step == NT)
    def _():
        out_ref[:, :EXTRA] = wg_ref[...]


def row_grads(both, gate, up, wg, after=()):
    clamp = lambda i: (jnp.minimum(i, NT - 1), 0)
    return pl.pallas_call(
        rows_kernel,
        grid=(NT + 1,),
        in_specs=[
            pl.BlockSpec((2, ROWS, FF), lambda i: (0, 0, 0)),
            pl.BlockSpec((TILE, FF), clamp),
            pl.BlockSpec((TILE, FF), clamp),
            pl.BlockSpec((ROWS, EXTRA), lambda i: (0, 0)),
        ]
        + [pl.BlockSpec(memory_space=pl.ANY)] * len(after),
        out_specs=pl.BlockSpec((ROWS, TILE), lambda i: (0, i)),
        out_shape=jax.ShapeDtypeStruct((ROWS, WIDE), BF),
        compiler_params=params(),
        cost_estimate=cost(4 * ROWS * D * FF, 21 * MB),
    )(both, gate, up, wg, *after)


def turned_kernel(scaled, deps, place_ref, x_ref, p_ref, *refs):
    send_ref, keep_ref, turned = refs[deps:]
    x = x_ref[...]
    if scaled:
        x = (p_ref[:, 0:1].astype(F32) * x.astype(F32)).astype(BF)
    turned[...] = x.T
    core = place_ref[8]
    for j in range(2):
        rows = slice(j * SUB, (j + 1) * SUB)
        far = pl.multiple_of((2 * j + 1 - core) * SUB, SUB)
        near = pl.multiple_of((2 * j + core) * SUB, SUB)
        send_ref[0, rows, :] = turned[pl.ds(far, SUB), :]
        keep_ref[0, rows, :] = turned[pl.ds(near, SUB), :]


def turned(place, x, p, scaled, after=()):
    last = (p.shape[1] // EXTRA) - 1
    send, keep = pl.pallas_call(
        functools.partial(turned_kernel, scaled, len(after)),
        grid_spec=pltpu.PrefetchScalarGridSpec(
            num_scalar_prefetch=1,
            grid=(NZ,),
            in_specs=[
                pl.BlockSpec((ROWS, ZB), lambda i, place: (0, i)),
                pl.BlockSpec((ROWS, EXTRA), lambda i, place: (0, last)),
            ]
            + [pl.BlockSpec(memory_space=pl.ANY)] * len(after),
            out_specs=[pl.BlockSpec((1, 2 * SUB, ROWS), lambda i, place: (i, 0, 0))] * 2,
            scratch_shapes=[pltpu.VMEM((ZB, ROWS), BF)],
        ),
        out_shape=[jax.ShapeDtypeStruct((NZ, 2 * SUB, ROWS), BF)] * 2,
        compiler_params=params(),
        cost_estimate=cost(ROWS * D, 8 * MB),
    )(place, x, p, *after)
    return keep, lax.ppermute(send, "dp", TO_CORE)


def combine_kernel(picks_ref, rows_ref, *refs):
    tokens_ref, weights_ref = refs[-2:]
    step = pl.program_id(0)

    @pl.when(step < NT)
    def _():
        both = picks_ref[0] + picks_ref[1]
        tokens_ref[...] = lax.dot_general(
            both, rows_ref[...], FIRST, preferred_element_type=F32
        ).astype(BF)

    @pl.when(step == NT)
    def _():
        found = [
            lax.dot_general(
                picks_ref[k], rows_ref[:, :EXTRA], FIRST, preferred_element_type=F32
            )
            for k in range(TOP)
        ]
        lane = lax.broadcasted_iota(jnp.int32, (TOK, EXTRA), 1)
        weights_ref[...] = jnp.where(lane == 0, found[0], found[1]).astype(BF)[:, :TOP]


def combine(picks, rows, after=()):
    return pl.pallas_call(
        combine_kernel,
        grid=(NT + 1,),
        in_specs=[
            pl.BlockSpec((TOP, ROWS, TOK), lambda i: (0, 0, 0)),
            pl.BlockSpec((ROWS, TILE), lambda i: (0, i)),
        ]
        + [pl.BlockSpec(memory_space=pl.ANY)] * len(after),
        out_specs=[
            pl.BlockSpec((TOK, TILE), lambda i: (0, jnp.minimum(i, NT - 1))),
            pl.BlockSpec((TOK, TOP), lambda i: (0, 0)),
        ],
        out_shape=[
            jax.ShapeDtypeStruct((TOK, D), BF),
            jax.ShapeDtypeStruct((TOK, TOP), BF),
        ],
        compiler_params=params(),
        cost_estimate=cost(2 * ROWS * TOK * D, 5 * MB),
    )(picks, rows, *after)


def moves(f):
    pairs = []
    for z in range(NZ):
        for x in range(2):
            for c in range(2):
                tz, tx, tc = f(z, x, c)
                pairs.append((z * 4 + x * 2 + c, (tz % NZ) * 4 + tx * 2 + tc))
    return pairs


TO_CORE = moves(lambda z, x, c: (z, x, 1 - c))
TO_UP = moves(lambda z, x, c: (z + 1, x, c))
TO_DOWN = moves(lambda z, x, c: (z - 1, x, c))
TO_X = moves(lambda z, x, c: (z, 1 - x, c))


def add(*parts):
    total = parts[0].astype(F32)
    for part in parts[1:]:
        total = total + part.astype(F32)
    return total.astype(BF)


def wide_kernel(place_ref, left_a, left_b, right_a, right_b, *refs):
    total = jnp.dot(left_a[0], right_a[0], preferred_element_type=F32)
    total = total + jnp.dot(left_b[0], right_b[0], preferred_element_type=F32)
    for k, out_ref in enumerate(refs[-2:]):

        @pl.when(pl.program_id(0) == k)
        def _():
            out_ref[...] = total.astype(BF)


def wide_parts(place, step, lefts, rights, after=()):
    left = pl.BlockSpec((1, 2 * SUB, ROWS), lambda i, place: (place[2 * step + i], 0, 0))
    right = pl.BlockSpec((1, ROWS, FF), lambda i, place: (i, 0, 0))
    return pl.pallas_call(
        wide_kernel,
        grid_spec=pltpu.PrefetchScalarGridSpec(
            num_scalar_prefetch=1,
            grid=(2,),
            in_specs=[left, left, right, right]
            + [pl.BlockSpec(memory_space=pl.ANY)] * len(after),
            out_specs=[pl.BlockSpec((2 * SUB, FF), lambda i, place: (0, 0))] * 2,
        ),
        out_shape=[jax.ShapeDtypeStruct((2 * SUB, FF), BF)] * 2,
        compiler_params=params(),
        cost_estimate=cost(16 * SUB * ROWS * FF, 8 * MB),
    )(place, *lefts, *rights, *after)


def down_kernel(place_ref, left_a, left_b, right_a, right_b, *refs):
    total = jnp.dot(left_a[0], right_a[...], preferred_element_type=F32)
    total = total + jnp.dot(left_b[0], right_b[...], preferred_element_type=F32)
    refs[-1][0] = total.astype(BF)


def down_parts(place, entry, lefts, rights, after=()):
    left = pl.BlockSpec((1, SUB, ROWS), lambda i, place: (i, place[entry], 0))
    right = pl.BlockSpec((ROWS, FF), lambda i, place: (0, 0))
    return pl.pallas_call(
        down_kernel,
        grid_spec=pltpu.PrefetchScalarGridSpec(
            num_scalar_prefetch=1,
            grid=(NZ,),
            in_specs=[left, left, right, right]
            + [pl.BlockSpec(memory_space=pl.ANY)] * len(after),
            out_specs=pl.BlockSpec((1, SUB, FF), lambda i, place: (i, 0, 0)),
        ),
        out_shape=jax.ShapeDtypeStruct((NZ, SUB, FF), BF),
        compiler_params=params(),
        cost_estimate=cost(16 * SUB * ROWS * FF, 8 * MB),
    )(place, *lefts, *rights, *after)


def around(up, down):
    return lax.ppermute(up, "dp", TO_UP), lax.ppermute(down, "dp", TO_DOWN)


def at_x(x, rows):
    return lax.dynamic_slice_in_dim(rows, x * SUB, SUB, 0)


def down_add(place, step, parts, moved):
    up = [lax.dynamic_index_in_dim(p, place[2 * step], 0, keepdims=False)[:, :HALF] for p in parts]
    down = [
        lax.dynamic_index_in_dim(p, place[2 * step + 1], 0, keepdims=False)[:, HALF:] for p in parts
    ]
    return add(*up, *moved[:1]), add(*down, *moved[1:])


PLACES = np.array(
    [
        [v for s in range(NZ) for v in ((z - 1 - s) % NZ, (z + 1 + s) % NZ)] + [c, x, 1 - x]
        for z in range(NZ)
        for x in range(2)
        for c in range(2)
    ],
    np.int32,
)


def exchange(rows):
    width = rows.shape[1]
    out = lax.all_to_all(
        rows.reshape(EXPERTS, CAP, width), "expert", split_axis=0, concat_axis=0, tiled=True
    )
    return out.reshape(ROWS, width)


def local(tokens, grad_out, routes, probs, w_gate, w_up, w_down):
    place = lax.dynamic_index_in_dim(jnp.asarray(PLACES), lax.axis_index("dp"), 0, keepdims=False)
    gate, up, down = w_gate[0], w_up[0], w_down[0]
    picks, send_tokens = place_tokens(routes, tokens)
    row_tokens = exchange(send_tokens)
    send_grads = place_grads(picks, probs, grad_out)
    row_grads_in = exchange(send_grads)
    hidden, active, slope = forward(row_tokens, gate, up)
    lefts = turned(place, row_tokens, row_tokens, False, after=(hidden,))
    hiddens = (hidden, lax.ppermute(hidden, "dp", TO_CORE))
    both, wg = backward(
        row_grads_in, down, hidden, active, slope, after=(lefts[0], lefts[1], hiddens[1])
    )
    boths = (both, lax.ppermute(both, "dp", TO_CORE))
    dlefts = turned(place, row_grads_in, row_grads_in, True, after=(both,))
    x = place[9]
    ring0 = wide_parts(place, 0, lefts, boths, after=dlefts[:1])
    moved0 = around(*ring0)
    far = down_parts(place, 10, dlefts, hiddens, after=ring0[:1])
    far_in = lax.ppermute(far, "dp", TO_X)
    parts1 = wide_parts(place, 1, lefts, boths, after=(far,))
    near = down_parts(place, 9, dlefts, hiddens, after=parts1[:1])
    ring1 = add(parts1[0], moved0[0]), add(parts1[1], moved0[1])
    moved1 = around(*ring1)
    sent_rows = row_grads(both, gate, up, wg, after=ring1 + (near,))
    returned = exchange(sent_rows)
    parts2 = wide_parts(place, 2, lefts, boths, after=(sent_rows,))
    down_pair = (near, far_in)
    down_moved0 = around(*down_add(place, 0, down_pair, ()))
    ring2 = add(parts2[0], moved1[0]), add(parts2[1], moved1[1])
    moved2 = around(*ring2)
    parts3 = wide_parts(place, 3, lefts, boths, after=ring2)
    down_moved1 = around(*down_add(place, 1, down_pair, down_moved0))
    down_moved2 = around(*down_add(place, 2, down_pair, down_moved1))
    down_grad = jnp.concatenate(down_add(place, 3, down_pair, down_moved2), axis=1)
    mine = [add(at_x(x, a), at_x(x, b)) for a, b in zip(parts3, moved2)]
    away = jnp.stack([add(at_x(1 - x, a), at_x(1 - x, b)) for a, b in zip(parts3, moved2)])
    came = lax.ppermute(away, "dp", TO_X)
    grad_tokens, grad_weights = combine(picks, returned, after=(away,))
    mine, grad_tokens = lax.optimization_barrier((mine, grad_tokens))
    grad_gate = add(mine[0], came[0])[None]
    grad_up = add(mine[1], came[1])[None]
    grad_down = down_grad[None]
    return (grad_tokens, grad_weights, grad_gate, grad_up, grad_down)


def solution(mesh):
    spec = P(("dp", "expert"), None)
    weight = P("expert", None, None)
    out = P("expert", "dp", None)
    return jax.shard_map(
        local,
        mesh=mesh,
        in_specs=(spec, spec, spec, spec, weight, weight, weight),
        out_specs=(spec, spec, out, out, out),
        check_vma=False,
    )
```

```python
import functools

import jax
import jax.numpy as jnp
import numpy as np
from jax import lax
from jax.experimental import pallas as pl
from jax.experimental.pallas import tpu as pltpu
from jax.sharding import PartitionSpec as P

D = 3584
FF = 1024
TOP = 2
CAP = 64
EXPERTS = 8
ROWS = EXPERTS * CAP
TOK = 128
EXTRA = 128
WIDE = D + EXTRA
TILE = 1792
NT = D // TILE
NZ = 4
ZB = D // NZ
SUB = ZB // 4
HALF = FF // 2
BF = jnp.bfloat16
F32 = jnp.float32
FIRST = (((0,), (0,)), ((), ()))
LAST = (((1,), (1,)), ((), ()))
MB = 1 << 20


def params(limit=60):
    return pltpu.CompilerParams(vmem_limit_bytes=limit * MB)


def cost(flops, nbytes, trans=0):
    return pl.CostEstimate(flops=flops, bytes_accessed=nbytes, transcendentals=trans)


SHORT = cost(1, 1)
LONG = cost(25_000_000_000, 1)
PRODUCT = cost(16 * SUB * ROWS * FF, 8 * MB)
WIDE_COSTS = (PRODUCT, PRODUCT, cost(14_000_000_000, 1), SHORT)


def place_kernel(routes_ref, tokens_ref, picks_ref, out_ref):
    @pl.when(pl.program_id(0) == 0)
    def _():
        routes = routes_ref[...]
        ids = lax.broadcasted_iota(jnp.int32, (TOK, EXPERTS), 1)
        first = (routes[:, 0:1] == ids).astype(F32).astype(BF)
        second = (routes[:, 1:2] == ids).astype(F32).astype(BF)
        row = lax.broadcasted_iota(jnp.int32, (TOK, TOK), 0)
        col = lax.broadcasted_iota(jnp.int32, (TOK, TOK), 1)
        before = (row < col).astype(F32).astype(BF)
        same = (row == col).astype(F32).astype(BF)
        rank = lax.dot_general(first + second, before, FIRST, preferred_element_type=F32)
        slot = lax.broadcasted_iota(jnp.int32, (CAP, TOK), 0).astype(F32)
        for k, named in enumerate((first, second)):
            named_t = lax.dot_general(named, same, FIRST, preferred_element_type=F32)
            for e in range(EXPERTS):
                hit = (slot == rank[e : e + 1, :]) & (named_t[e : e + 1, :] > 0.5)
                picks_ref[k, e * CAP : (e + 1) * CAP, :] = hit.astype(F32).astype(BF)

    both = picks_ref[0] + picks_ref[1]
    out_ref[...] = jnp.dot(both, tokens_ref[...], preferred_element_type=F32).astype(BF)


def place_tokens(routes, tokens):
    return pl.pallas_call(
        place_kernel,
        grid=(NT,),
        in_specs=[
            pl.BlockSpec((TOK, TOP), lambda i: (0, 0)),
            pl.BlockSpec((TOK, TILE), lambda i: (0, i)),
        ],
        out_specs=[
            pl.BlockSpec((TOP, ROWS, TOK), lambda i: (0, 0, 0)),
            pl.BlockSpec((ROWS, TILE), lambda i: (0, i)),
        ],
        out_shape=[
            jax.ShapeDtypeStruct((TOP, ROWS, TOK), BF),
            jax.ShapeDtypeStruct((ROWS, D), BF),
        ],
        compiler_params=params(),
        cost_estimate=cost(2 * ROWS * TOK * D, 5 * MB),
    )(routes, tokens)


def grads_kernel(picks_ref, probs_ref, grads_ref, out_ref):
    step = pl.program_id(0)

    @pl.when(step < NT)
    def _():
        both = picks_ref[0] + picks_ref[1]
        out_ref[...] = jnp.dot(both, grads_ref[...], preferred_element_type=F32).astype(BF)

    @pl.when(step == NT)
    def _():
        probs = probs_ref[...].astype(F32)
        p0 = jnp.broadcast_to(probs[:, 0:1], (TOK, EXTRA)).astype(BF)
        p1 = jnp.broadcast_to(probs[:, 1:2], (TOK, EXTRA)).astype(BF)
        spread = jnp.dot(picks_ref[0], p0, preferred_element_type=F32)
        spread = spread + jnp.dot(picks_ref[1], p1, preferred_element_type=F32)
        out_ref[:, :EXTRA] = spread.astype(BF)


def place_grads(picks, probs, grads):
    return pl.pallas_call(
        grads_kernel,
        grid=(NT + 1,),
        in_specs=[
            pl.BlockSpec((TOP, ROWS, TOK), lambda i: (0, 0, 0)),
            pl.BlockSpec((TOK, TOP), lambda i: (0, 0)),
            pl.BlockSpec((TOK, TILE), lambda i: (0, jnp.minimum(i, NT - 1))),
        ],
        out_specs=pl.BlockSpec((ROWS, TILE), lambda i: (0, i)),
        out_shape=jax.ShapeDtypeStruct((ROWS, WIDE), BF),
        compiler_params=params(),
        cost_estimate=cost(2 * ROWS * TOK * D, 5 * MB),
    )(picks, probs, grads)


def forward_kernel(x_ref, gate_ref, up_ref, hidden_ref, active_ref, slope_ref):
    x = x_ref[...]
    gate = jnp.dot(x, gate_ref[...], preferred_element_type=F32)
    up = jnp.dot(x, up_ref[...], preferred_element_type=F32)
    s = jax.nn.sigmoid(gate)
    active = gate * s
    hidden_ref[...] = (active * up).astype(BF)
    active_ref[...] = active
    slope_ref[...] = up * s * (1.0 + gate * (1.0 - s))


def forward(x, gate, up):
    n = 256
    return pl.pallas_call(
        forward_kernel,
        grid=(FF // n,),
        in_specs=[
            pl.BlockSpec((ROWS, D), lambda i: (0, 0)),
            pl.BlockSpec((D, n), lambda i: (0, i)),
            pl.BlockSpec((D, n), lambda i: (0, i)),
        ],
        out_specs=[pl.BlockSpec((ROWS, n), lambda i: (0, i))] * 3,
        out_shape=[
            jax.ShapeDtypeStruct((ROWS, FF), BF),
            jax.ShapeDtypeStruct((ROWS, FF), F32),
            jax.ShapeDtypeStruct((ROWS, FF), F32),
        ],
        compiler_params=params(),
        cost_estimate=cost(4 * ROWS * D * FF, 23 * MB, ROWS * FF),
    )(x, gate, up)


def backward_kernel(g_ref, down_ref, hidden_ref, active_ref, slope_ref, *refs):
    both_ref, wg_ref, total = refs[-3:]
    step = pl.program_id(0)
    back = jnp.dot(g_ref[:, :D], down_ref[...], preferred_element_type=F32)
    part = jnp.sum(back * hidden_ref[...].astype(F32), axis=1, keepdims=True)

    @pl.when(step == 0)
    def _():
        total[...] = jnp.zeros_like(total)

    total[...] += jnp.broadcast_to(part, total.shape)
    scaled = g_ref[:, D : D + 1].astype(F32) * back
    both_ref[0] = (scaled * slope_ref[...]).astype(BF)
    both_ref[1] = (scaled * active_ref[...]).astype(BF)
    wg_ref[...] = total[...].astype(BF)


def backward(g, down, hidden, active, slope, after=()):
    n = 512
    tile = pl.BlockSpec((ROWS, n), lambda i: (0, i))
    return pl.pallas_call(
        backward_kernel,
        grid=(FF // n,),
        in_specs=[
            pl.BlockSpec((ROWS, WIDE), lambda i: (0, 0)),
            pl.BlockSpec((D, n), lambda i: (0, i)),
            tile,
            tile,
            tile,
        ]
        + [pl.BlockSpec(memory_space=pl.ANY)] * len(after),
        out_specs=[
            pl.BlockSpec((2, ROWS, n), lambda i: (0, 0, i)),
            pl.BlockSpec((ROWS, EXTRA), lambda i: (0, 0)),
        ],
        out_shape=[
            jax.ShapeDtypeStruct((2, ROWS, FF), BF),
            jax.ShapeDtypeStruct((ROWS, EXTRA), BF),
        ],
        scratch_shapes=[pltpu.VMEM((ROWS, EXTRA), F32)],
        compiler_params=params(),
        cost_estimate=cost(2 * ROWS * D * FF, 18 * MB),
    )(g, down, hidden, active, slope, *after)


def rows_kernel(both_ref, gate_ref, up_ref, wg_ref, *refs):
    out_ref = refs[-1]
    step = pl.program_id(0)

    @pl.when(step < NT)
    def _():
        grad = lax.dot_general(both_ref[0], gate_ref[...], LAST, preferred_element_type=F32)
        grad = grad + lax.dot_general(both_ref[1], up_ref[...], LAST, preferred_element_type=F32)
        out_ref[...] = grad.astype(BF)

    @pl.when(step == NT)
    def _():
        out_ref[:, :EXTRA] = wg_ref[...]


def row_grads(both, gate, up, wg, after=()):
    clamp = lambda i: (jnp.minimum(i, NT - 1), 0)
    return pl.pallas_call(
        rows_kernel,
        grid=(NT + 1,),
        in_specs=[
            pl.BlockSpec((2, ROWS, FF), lambda i: (0, 0, 0)),
            pl.BlockSpec((TILE, FF), clamp),
            pl.BlockSpec((TILE, FF), clamp),
            pl.BlockSpec((ROWS, EXTRA), lambda i: (0, 0)),
        ]
        + [pl.BlockSpec(memory_space=pl.ANY)] * len(after),
        out_specs=pl.BlockSpec((ROWS, TILE), lambda i: (0, i)),
        out_shape=jax.ShapeDtypeStruct((ROWS, WIDE), BF),
        compiler_params=params(),
        cost_estimate=SHORT,
    )(both, gate, up, wg, *after)


def turned_kernel(scaled, deps, place_ref, x_ref, p_ref, *refs):
    send_ref, keep_ref, turned = refs[deps:]
    rows_in = x_ref[...]
    if scaled:
        rows_in = (p_ref[:, 0:1].astype(F32) * rows_in.astype(F32)).astype(BF)
    turned[...] = rows_in.T
    core, x = place_ref[8], place_ref[9]
    for j in range(2):
        rows = slice(j * SUB, (j + 1) * SUB)
        block = 2 * (x + j - 2 * x * j)
        far = pl.multiple_of((block + 1 - core) * SUB, SUB)
        near = pl.multiple_of((block + core) * SUB, SUB)
        send_ref[0, rows, :] = turned[pl.ds(far, SUB), :]
        keep_ref[0, rows, :] = turned[pl.ds(near, SUB), :]


def turned(place, x, p, scaled, after=()):
    last = (p.shape[1] // EXTRA) - 1
    send, keep = pl.pallas_call(
        functools.partial(turned_kernel, scaled, len(after)),
        grid_spec=pltpu.PrefetchScalarGridSpec(
            num_scalar_prefetch=1,
            grid=(NZ,),
            in_specs=[
                pl.BlockSpec((ROWS, ZB), lambda i, place: (0, i)),
                pl.BlockSpec((ROWS, EXTRA), lambda i, place: (0, last)),
            ]
            + [pl.BlockSpec(memory_space=pl.ANY)] * len(after),
            out_specs=[pl.BlockSpec((1, 2 * SUB, ROWS), lambda i, place: (i, 0, 0))] * 2,
            scratch_shapes=[pltpu.VMEM((ZB, ROWS), BF)],
        ),
        out_shape=[jax.ShapeDtypeStruct((NZ, 2 * SUB, ROWS), BF)] * 2,
        compiler_params=params(),
        cost_estimate=cost(ROWS * D, 8 * MB),
    )(place, x, p, *after)
    return keep, lax.ppermute(send, "dp", TO_CORE)


def combine_kernel(picks_ref, rows_ref, *refs):
    tokens_ref, weights_ref = refs[-2:]
    step = pl.program_id(0)

    @pl.when(step < NT)
    def _():
        both = picks_ref[0] + picks_ref[1]
        tokens_ref[...] = lax.dot_general(
            both, rows_ref[...], FIRST, preferred_element_type=F32
        ).astype(BF)

    @pl.when(step == NT)
    def _():
        found = [
            lax.dot_general(
                picks_ref[k], rows_ref[:, :EXTRA], FIRST, preferred_element_type=F32
            )
            for k in range(TOP)
        ]
        lane = lax.broadcasted_iota(jnp.int32, (TOK, EXTRA), 1)
        weights_ref[...] = jnp.where(lane == 0, found[0], found[1]).astype(BF)[:, :TOP]


def combine(picks, rows, after=()):
    return pl.pallas_call(
        combine_kernel,
        grid=(NT + 1,),
        in_specs=[
            pl.BlockSpec((TOP, ROWS, TOK), lambda i: (0, 0, 0)),
            pl.BlockSpec((ROWS, TILE), lambda i: (0, i)),
        ]
        + [pl.BlockSpec(memory_space=pl.ANY)] * len(after),
        out_specs=[
            pl.BlockSpec((TOK, TILE), lambda i: (0, jnp.minimum(i, NT - 1))),
            pl.BlockSpec((TOK, TOP), lambda i: (0, 0)),
        ],
        out_shape=[
            jax.ShapeDtypeStruct((TOK, D), BF),
            jax.ShapeDtypeStruct((TOK, TOP), BF),
        ],
        compiler_params=params(),
        cost_estimate=LONG,
    )(picks, rows, *after)


def moves(f):
    pairs = []
    for z in range(NZ):
        for x in range(2):
            for c in range(2):
                tz, tx, tc = f(z, x, c)
                pairs.append((z * 4 + x * 2 + c, (tz % NZ) * 4 + tx * 2 + tc))
    return pairs


TO_CORE = moves(lambda z, x, c: (z, x, 1 - c))
TO_UP = moves(lambda z, x, c: (z + 1, x, c))
TO_DOWN = moves(lambda z, x, c: (z - 1, x, c))
TO_X = moves(lambda z, x, c: (z, 1 - x, c))


def add(*parts):
    total = parts[0].astype(F32)
    for part in parts[1:]:
        total = total + part.astype(F32)
    return total.astype(BF)


def wide_kernel(place_ref, left_a, left_b, right_a, right_b, *refs):
    total = jnp.dot(left_a[0], right_a[0], preferred_element_type=F32)
    total = total + jnp.dot(left_b[0], right_b[0], preferred_element_type=F32)
    for k, out_ref in enumerate(refs[-2:]):

        @pl.when(pl.program_id(0) == k)
        def _():
            out_ref[...] = total.astype(BF)


def wide_parts(place, step, lefts, rights, after=()):
    left = pl.BlockSpec((1, 2 * SUB, ROWS), lambda i, place: (place[2 * step + i], 0, 0))
    right = pl.BlockSpec((1, ROWS, FF), lambda i, place: (i, 0, 0))
    return pl.pallas_call(
        wide_kernel,
        grid_spec=pltpu.PrefetchScalarGridSpec(
            num_scalar_prefetch=1,
            grid=(2,),
            in_specs=[left, left, right, right]
            + [pl.BlockSpec(memory_space=pl.ANY)] * len(after),
            out_specs=[pl.BlockSpec((2 * SUB, FF), lambda i, place: (0, 0))] * 2,
        ),
        out_shape=[jax.ShapeDtypeStruct((2 * SUB, FF), BF)] * 2,
        compiler_params=params(),
        cost_estimate=WIDE_COSTS[step],
    )(place, *lefts, *rights, *after)


def down_kernel(place_ref, left_a, left_b, right_a, right_b, *refs):
    total = jnp.dot(left_a[0], right_a[...], preferred_element_type=F32)
    total = total + jnp.dot(left_b[0], right_b[...], preferred_element_type=F32)
    refs[-1][0] = total.astype(BF)


def down_parts(place, which, lefts, rights, after=()):
    left = pl.BlockSpec((1, SUB, ROWS), lambda i, place: (place[i], which, 0))
    right = pl.BlockSpec((ROWS, HALF), lambda i, place: (0, i % 2))
    return pl.pallas_call(
        down_kernel,
        grid_spec=pltpu.PrefetchScalarGridSpec(
            num_scalar_prefetch=1,
            grid=(2 * NZ,),
            in_specs=[left, left, right, right]
            + [pl.BlockSpec(memory_space=pl.ANY)] * len(after),
            out_specs=pl.BlockSpec((1, SUB, HALF), lambda i, place: (i, 0, 0)),
        ),
        out_shape=jax.ShapeDtypeStruct((2 * NZ, SUB, HALF), BF),
        compiler_params=params(),
        cost_estimate=cost(16 * SUB * ROWS * FF, 8 * MB),
    )(place, *lefts, *rights, *after)


def around(up, down):
    return lax.ppermute(up, "dp", TO_UP), lax.ppermute(down, "dp", TO_DOWN)


def wide_add_kernel(part_up, part_down, up_ref, down_ref, *refs):
    refs[-2][...] = (part_up[...].astype(F32) + up_ref[...].astype(F32)).astype(BF)
    refs[-1][...] = (part_down[...].astype(F32) + down_ref[...].astype(F32)).astype(BF)


def wide_add(parts, moved, after=()):
    spec = pl.BlockSpec((SUB, FF), lambda i: (i, 0))
    return pl.pallas_call(
        wide_add_kernel,
        grid=(2,),
        in_specs=[spec] * 4 + [pl.BlockSpec(memory_space=pl.ANY)] * len(after),
        out_specs=[spec] * 2,
        out_shape=[jax.ShapeDtypeStruct((2 * SUB, FF), BF)] * 2,
        compiler_params=params(),
        cost_estimate=SHORT,
    )(*parts, *moved, *after)


def wide_last_kernel(part_up, part_down, up_ref, down_ref, *refs):
    mine_ref, away_ref = refs[-2:]
    sums = [
        (a[...].astype(F32) + b[...].astype(F32)).astype(BF)
        for a, b in ((part_up, up_ref), (part_down, down_ref))
    ]
    for step, out_ref in enumerate((away_ref, mine_ref)):

        @pl.when(pl.program_id(0) == step)
        def _():
            out_ref[0] = sums[0]
            out_ref[1] = sums[1]


def wide_last(parts, moved, after=()):
    spec = pl.BlockSpec((SUB, FF), lambda i: (1 - i, 0))
    out = pl.BlockSpec((2, SUB, FF), lambda i: (0, 0, 0))
    return pl.pallas_call(
        wide_last_kernel,
        grid=(2,),
        in_specs=[spec] * 4 + [pl.BlockSpec(memory_space=pl.ANY)] * len(after),
        out_specs=[out] * 2,
        out_shape=[jax.ShapeDtypeStruct((2, SUB, FF), BF)] * 2,
        compiler_params=params(),
        cost_estimate=SHORT,
    )(*parts, *moved, *after)


def down_add_kernel(moved, near_ref, far_ref, *refs):
    sums = [near_ref[k].astype(F32) + far_ref[k].astype(F32) for k in range(2)]
    if moved:
        sums = [a + ref[...].astype(F32) for a, ref in zip(sums, refs)]
    if len(refs[-1].shape) == 2 and refs[-1].shape[1] == FF:
        refs[-1][:, :HALF] = sums[0].astype(BF)
        refs[-1][:, HALF:] = sums[1].astype(BF)
    else:
        refs[-2][...] = sums[0].astype(BF)
        refs[-1][...] = sums[1].astype(BF)


def down_add(step, parts, moved=(), after=()):
    pair = pl.BlockSpec((2, SUB, HALF), lambda i: (step, 0, 0))
    one = pl.BlockSpec((SUB, HALF), lambda i: (0, 0))
    whole = pl.BlockSpec((SUB, FF), lambda i: (0, 0))
    last = step == NZ - 1
    return pl.pallas_call(
        functools.partial(down_add_kernel, len(moved) > 0),
        grid=(1,),
        in_specs=[pair] * 2
        + [one] * len(moved)
        + [pl.BlockSpec(memory_space=pl.ANY)] * len(after),
        out_specs=[whole] if last else [one] * 2,
        out_shape=[jax.ShapeDtypeStruct((SUB, FF), BF)]
        if last
        else [jax.ShapeDtypeStruct((SUB, HALF), BF)] * 2,
        compiler_params=params(),
        cost_estimate=LONG if step == 1 else SHORT,
    )(*parts, *moved, *after)


PLACES = np.array(
    [
        [v for s in range(NZ) for v in ((z - 1 - s) % NZ, (z + 1 + s) % NZ)] + [c, x]
        for z in range(NZ)
        for x in range(2)
        for c in range(2)
    ],
    np.int32,
)


def exchange(rows):
    width = rows.shape[1]
    out = lax.all_to_all(
        rows.reshape(EXPERTS, CAP, width), "expert", split_axis=0, concat_axis=0, tiled=True
    )
    return out.reshape(ROWS, width)


def local(tokens, grad_out, routes, probs, w_gate, w_up, w_down):
    place = lax.dynamic_slice(PLACES.reshape(-1), (10 * lax.axis_index("dp"),), (10,))
    gate, up, down = w_gate[0], w_up[0], w_down[0]
    picks, send_tokens = place_tokens(routes, tokens)
    row_tokens = exchange(send_tokens)
    send_grads = place_grads(picks, probs, grad_out)
    row_grads_in = exchange(send_grads)
    hidden, active, slope = forward(row_tokens, gate, up)
    lefts = turned(place, row_tokens, row_tokens, False, after=(hidden,))
    hiddens = (hidden, lax.ppermute(hidden, "dp", TO_CORE))
    both, wg = backward(
        row_grads_in, down, hidden, active, slope, after=(lefts[0], lefts[1], hiddens[1])
    )
    boths = (both, lax.ppermute(both, "dp", TO_CORE))
    dlefts = turned(place, row_grads_in, row_grads_in, True, after=(both,))
    ring0 = wide_parts(place, 0, lefts, boths, after=dlefts[:1])
    moved0 = around(*ring0)
    far = down_parts(place, 1, dlefts, hiddens, after=ring0[:1])
    far_in = lax.ppermute(far, "dp", TO_X)
    parts1 = wide_parts(place, 1, lefts, boths, after=(far,))
    near = down_parts(place, 0, dlefts, hiddens, after=parts1[:1])
    ring1 = wide_add(parts1, moved0, after=(near,))
    moved1 = around(*ring1)
    sent_rows = row_grads(both, gate, up, wg, after=ring1)
    returned = exchange(sent_rows)
    parts2 = wide_parts(place, 2, lefts, boths, after=(sent_rows,))
    down_pair = (near, far_in)
    down_ring0 = down_add(0, down_pair, after=parts2[:1])
    down_moved0 = around(*down_ring0)
    ring2 = wide_add(parts2, moved1, after=down_ring0)
    moved2 = around(*ring2)
    parts3 = wide_parts(place, 3, lefts, boths, after=ring2)
    down_ring1 = down_add(1, down_pair, down_moved0, after=parts3[:1])
    down_moved1 = around(*down_ring1)
    mine, away = wide_last(parts3, moved2, after=down_ring1)
    came = lax.ppermute(away, "dp", TO_X)
    down_ring2 = down_add(2, down_pair, down_moved1, after=(away,))
    down_moved2 = around(*down_ring2)
    grad_tokens, grad_weights = combine(picks, returned, after=down_ring2)
    (down_grad,) = down_add(3, down_pair, down_moved2, after=(grad_tokens,))
    mine, down_grad = lax.optimization_barrier((mine, down_grad))
    grad_gate = add(mine[0], came[0])[None]
    grad_up = add(mine[1], came[1])[None]
    grad_down = down_grad[None]
    return (grad_tokens, grad_weights, grad_gate, grad_up, grad_down)


def solution(mesh):
    spec = P(("dp", "expert"), None)
    weight = P("expert", None, None)
    out = P("expert", "dp", None)
    return jax.shard_map(
        local,
        mesh=mesh,
        in_specs=(spec, spec, spec, spec, weight, weight, weight),
        out_specs=(spec, spec, out, out, out),
        check_vma=False,
    )
```

```python
import functools

import jax
import jax.numpy as jnp
import numpy as np
from jax import lax
from jax.experimental import pallas as pl
from jax.experimental.pallas import tpu as pltpu
from jax.sharding import PartitionSpec as P

D = 3584
FF = 1024
TOP = 2
CAP = 64
EXPERTS = 8
ROWS = EXPERTS * CAP
TOK = 128
EXTRA = 128
WIDE = D + EXTRA
TILE = 1792
NT = D // TILE
NZ = 4
ZB = D // NZ
SUB = ZB // 4
HALF = FF // 2
BF = jnp.bfloat16
F32 = jnp.float32
FIRST = (((0,), (0,)), ((), ()))
LAST = (((1,), (1,)), ((), ()))
MB = 1 << 20


def params(limit=63):
    return pltpu.CompilerParams(vmem_limit_bytes=limit * MB)


def cost(flops, nbytes, trans=0):
    return pl.CostEstimate(flops=flops, bytes_accessed=nbytes, transcendentals=trans)


SHORT = cost(1, 1)
LONG = cost(25_000_000_000, 1)
PRODUCT = cost(16 * SUB * ROWS * FF, 8 * MB)
WIDE_COSTS = (PRODUCT, PRODUCT, cost(14_000_000_000, 1), SHORT)


def place_kernel(routes_ref, tokens_ref, picks_ref, out_ref):
    @pl.when(pl.program_id(0) == 0)
    def _():
        ids = lax.broadcasted_iota(jnp.int32, (EXPERTS, TOK), 0)
        named = [(routes_ref[k : k + 1, :] == ids).astype(F32) for k in range(TOP)]
        row = lax.broadcasted_iota(jnp.int32, (TOK, TOK), 0)
        col = lax.broadcasted_iota(jnp.int32, (TOK, TOK), 1)
        before = (row < col).astype(F32).astype(BF)
        rank = jnp.dot((named[0] + named[1]).astype(BF), before, preferred_element_type=F32)
        slot = lax.broadcasted_iota(jnp.int32, (CAP, TOK), 0).astype(F32)
        for k in range(TOP):
            for e in range(EXPERTS):
                hit = (slot == rank[e : e + 1, :]) & (named[k][e : e + 1, :] > 0.5)
                picks_ref[k, e * CAP : (e + 1) * CAP, :] = hit.astype(F32).astype(BF)

    both = picks_ref[0] + picks_ref[1]
    out_ref[...] = jnp.dot(both, tokens_ref[...], preferred_element_type=F32).astype(BF)


def place_tokens(routes, tokens):
    return pl.pallas_call(
        place_kernel,
        grid=(NT,),
        in_specs=[
            pl.BlockSpec((TOP, TOK), lambda i: (0, 0)),
            pl.BlockSpec((TOK, TILE), lambda i: (0, i)),
        ],
        out_specs=[
            pl.BlockSpec((TOP, ROWS, TOK), lambda i: (0, 0, 0)),
            pl.BlockSpec((ROWS, TILE), lambda i: (0, i)),
        ],
        out_shape=[
            jax.ShapeDtypeStruct((TOP, ROWS, TOK), BF),
            jax.ShapeDtypeStruct((ROWS, D), BF),
        ],
        compiler_params=params(),
        cost_estimate=cost(2 * ROWS * TOK * D, 5 * MB),
    )(routes.T, tokens)


def grads_kernel(picks_ref, probs_ref, grads_ref, out_ref):
    step = pl.program_id(0)

    @pl.when(step < NT)
    def _():
        both = picks_ref[0] + picks_ref[1]
        out_ref[...] = jnp.dot(both, grads_ref[...], preferred_element_type=F32).astype(BF)

    @pl.when(step == NT)
    def _():
        held = picks_ref[0] * probs_ref[0:1, :] + picks_ref[1] * probs_ref[1:2, :]
        ones = jnp.ones((TOK, EXTRA), BF)
        spread = jnp.dot(held, ones, preferred_element_type=F32)
        out_ref[:, :EXTRA] = spread.astype(BF)


def place_grads(picks, probs, grads):
    return pl.pallas_call(
        grads_kernel,
        grid=(NT + 1,),
        in_specs=[
            pl.BlockSpec((TOP, ROWS, TOK), lambda i: (0, 0, 0)),
            pl.BlockSpec((TOP, TOK), lambda i: (0, 0)),
            pl.BlockSpec((TOK, TILE), lambda i: (0, jnp.minimum(i, NT - 1))),
        ],
        out_specs=pl.BlockSpec((ROWS, TILE), lambda i: (0, i)),
        out_shape=jax.ShapeDtypeStruct((ROWS, WIDE), BF),
        compiler_params=params(),
        cost_estimate=cost(2 * ROWS * TOK * D, 5 * MB),
    )(picks, probs.T, grads)


def forward_kernel(x_ref, gate_ref, up_ref, hidden_ref, active_ref, slope_ref):
    x = x_ref[...]
    gate = jnp.dot(x, gate_ref[...], preferred_element_type=F32)
    up = jnp.dot(x, up_ref[...], preferred_element_type=F32)
    s = jax.nn.sigmoid(gate)
    active = gate * s
    hidden_ref[...] = (active * up).astype(BF)
    active_ref[...] = active
    slope_ref[...] = up * s * (1.0 + gate * (1.0 - s))


def forward(x, gate, up):
    n = 256
    return pl.pallas_call(
        forward_kernel,
        grid=(FF // n,),
        in_specs=[
            pl.BlockSpec((ROWS, D), lambda i: (0, 0)),
            pl.BlockSpec((D, n), lambda i: (0, i)),
            pl.BlockSpec((D, n), lambda i: (0, i)),
        ],
        out_specs=[pl.BlockSpec((ROWS, n), lambda i: (0, i))] * 3,
        out_shape=[
            jax.ShapeDtypeStruct((ROWS, FF), BF),
            jax.ShapeDtypeStruct((ROWS, FF), F32),
            jax.ShapeDtypeStruct((ROWS, FF), F32),
        ],
        compiler_params=params(),
        cost_estimate=cost(4 * ROWS * D * FF, 23 * MB, ROWS * FF),
    )(x, gate, up)


def backward_kernel(g_ref, down_ref, hidden_ref, active_ref, slope_ref, *refs):
    both_ref, wg_ref, total = refs[-3:]
    step = pl.program_id(0)
    back = jnp.dot(g_ref[:, :D], down_ref[...], preferred_element_type=F32)
    part = jnp.sum(back * hidden_ref[...].astype(F32), axis=1, keepdims=True)

    @pl.when(step == 0)
    def _():
        total[...] = jnp.zeros_like(total)

    total[...] += jnp.broadcast_to(part, total.shape)
    scaled = g_ref[:, D : D + 1].astype(F32) * back
    both_ref[0] = (scaled * slope_ref[...]).astype(BF)
    both_ref[1] = (scaled * active_ref[...]).astype(BF)
    wg_ref[...] = total[...].astype(BF)


def backward(g, down, hidden, active, slope, after=()):
    n = 512
    tile = pl.BlockSpec((ROWS, n), lambda i: (0, i))
    return pl.pallas_call(
        backward_kernel,
        grid=(FF // n,),
        in_specs=[
            pl.BlockSpec((ROWS, WIDE), lambda i: (0, 0)),
            pl.BlockSpec((D, n), lambda i: (0, i)),
            tile,
            tile,
            tile,
        ]
        + [pl.BlockSpec(memory_space=pl.ANY)] * len(after),
        out_specs=[
            pl.BlockSpec((2, ROWS, n), lambda i: (0, 0, i)),
            pl.BlockSpec((ROWS, EXTRA), lambda i: (0, 0)),
        ],
        out_shape=[
            jax.ShapeDtypeStruct((2, ROWS, FF), BF),
            jax.ShapeDtypeStruct((ROWS, EXTRA), BF),
        ],
        scratch_shapes=[pltpu.VMEM((ROWS, EXTRA), F32)],
        compiler_params=params(),
        cost_estimate=cost(2 * ROWS * D * FF, 18 * MB),
    )(g, down, hidden, active, slope, *after)


def rows_kernel(both_ref, gate_ref, up_ref, wg_ref, *refs):
    out_ref = refs[-1]
    step = pl.program_id(0)

    @pl.when(step < NT)
    def _():
        grad = lax.dot_general(both_ref[0], gate_ref[...], LAST, preferred_element_type=F32)
        grad = grad + lax.dot_general(both_ref[1], up_ref[...], LAST, preferred_element_type=F32)
        out_ref[...] = grad.astype(BF)

    @pl.when(step == NT)
    def _():
        out_ref[:, :EXTRA] = wg_ref[...]


def row_grads(both, gate, up, wg, after=()):
    clamp = lambda i: (jnp.minimum(i, NT - 1), 0)
    return pl.pallas_call(
        rows_kernel,
        grid=(NT + 1,),
        in_specs=[
            pl.BlockSpec((2, ROWS, FF), lambda i: (0, 0, 0)),
            pl.BlockSpec((TILE, FF), clamp),
            pl.BlockSpec((TILE, FF), clamp),
            pl.BlockSpec((ROWS, EXTRA), lambda i: (0, 0)),
        ]
        + [pl.BlockSpec(memory_space=pl.ANY)] * len(after),
        out_specs=pl.BlockSpec((ROWS, TILE), lambda i: (0, i)),
        out_shape=jax.ShapeDtypeStruct((ROWS, WIDE), BF),
        compiler_params=params(),
        cost_estimate=SHORT,
    )(both, gate, up, wg, *after)


def turned_kernel(scaled, deps, place_ref, x_ref, p_ref, *refs):
    send_ref, keep_ref, turned = refs[deps:]
    rows_in = x_ref[...]
    if scaled:
        rows_in = (p_ref[:, 0:1].astype(F32) * rows_in.astype(F32)).astype(BF)
    turned[...] = rows_in.T
    core, x = place_ref[8], place_ref[9]
    for j in range(2):
        rows = slice(j * SUB, (j + 1) * SUB)
        block = 2 * (x + j - 2 * x * j)
        far = pl.multiple_of((block + 1 - core) * SUB, SUB)
        near = pl.multiple_of((block + core) * SUB, SUB)
        send_ref[0, rows, :] = turned[pl.ds(far, SUB), :]
        keep_ref[0, rows, :] = turned[pl.ds(near, SUB), :]


def turned(place, x, p, scaled, after=()):
    last = (p.shape[1] // EXTRA) - 1
    send, keep = pl.pallas_call(
        functools.partial(turned_kernel, scaled, len(after)),
        grid_spec=pltpu.PrefetchScalarGridSpec(
            num_scalar_prefetch=1,
            grid=(NZ,),
            in_specs=[
                pl.BlockSpec((ROWS, ZB), lambda i, place: (0, i)),
                pl.BlockSpec((ROWS, EXTRA), lambda i, place: (0, last)),
            ]
            + [pl.BlockSpec(memory_space=pl.ANY)] * len(after),
            out_specs=[pl.BlockSpec((1, 2 * SUB, ROWS), lambda i, place: (i, 0, 0))] * 2,
            scratch_shapes=[pltpu.VMEM((ZB, ROWS), BF)],
        ),
        out_shape=[jax.ShapeDtypeStruct((NZ, 2 * SUB, ROWS), BF)] * 2,
        compiler_params=params(),
        cost_estimate=cost(ROWS * D, 8 * MB),
    )(place, x, p, *after)
    return keep, lax.ppermute(send, "dp", TO_CORE)


def combine_kernel(picks_ref, rows_ref, *refs):
    tokens_ref, weights_ref = refs[-2:]
    step = pl.program_id(0)

    @pl.when(step < NT)
    def _():
        both = picks_ref[0] + picks_ref[1]
        tokens_ref[...] = lax.dot_general(
            both, rows_ref[...], FIRST, preferred_element_type=F32
        ).astype(BF)

    @pl.when(step == NT)
    def _():
        for k in range(TOP):
            found = lax.dot_general(
                rows_ref[:, :EXTRA], picks_ref[k], FIRST, preferred_element_type=F32
            )
            weights_ref[k : k + 1, :] = found[0:1].astype(BF)


def combine(picks, rows, after=()):
    return pl.pallas_call(
        combine_kernel,
        grid=(NT + 1,),
        in_specs=[
            pl.BlockSpec((TOP, ROWS, TOK), lambda i: (0, 0, 0)),
            pl.BlockSpec((ROWS, TILE), lambda i: (0, i)),
        ]
        + [pl.BlockSpec(memory_space=pl.ANY)] * len(after),
        out_specs=[
            pl.BlockSpec((TOK, TILE), lambda i: (0, jnp.minimum(i, NT - 1))),
            pl.BlockSpec((TOP, TOK), lambda i: (0, 0)),
        ],
        out_shape=[
            jax.ShapeDtypeStruct((TOK, D), BF),
            jax.ShapeDtypeStruct((TOP, TOK), BF),
        ],
        compiler_params=params(),
        cost_estimate=LONG,
    )(picks, rows, *after)


def moves(f):
    pairs = []
    for z in range(NZ):
        for x in range(2):
            for c in range(2):
                tz, tx, tc = f(z, x, c)
                pairs.append((z * 4 + x * 2 + c, (tz % NZ) * 4 + tx * 2 + tc))
    return pairs


TO_CORE = moves(lambda z, x, c: (z, x, 1 - c))
TO_UP = moves(lambda z, x, c: (z + 1, x, c))
TO_DOWN = moves(lambda z, x, c: (z - 1, x, c))
TO_X = moves(lambda z, x, c: (z, 1 - x, c))


def add(*parts):
    total = parts[0].astype(F32)
    for part in parts[1:]:
        total = total + part.astype(F32)
    return total.astype(BF)


def wide_kernel(place_ref, left_a, left_b, right_a, right_b, *refs):
    total = jnp.dot(left_a[0], right_a[0], preferred_element_type=F32)
    total = total + jnp.dot(left_b[0], right_b[0], preferred_element_type=F32)
    for k, out_ref in enumerate(refs[-2:]):

        @pl.when(pl.program_id(0) == k)
        def _():
            out_ref[...] = total.astype(BF)


def wide_parts(place, step, lefts, rights, after=()):
    left = pl.BlockSpec((1, 2 * SUB, ROWS), lambda i, place: (place[2 * step + i], 0, 0))
    right = pl.BlockSpec((1, ROWS, FF), lambda i, place: (i, 0, 0))
    return pl.pallas_call(
        wide_kernel,
        grid_spec=pltpu.PrefetchScalarGridSpec(
            num_scalar_prefetch=1,
            grid=(2,),
            in_specs=[left, left, right, right]
            + [pl.BlockSpec(memory_space=pl.ANY)] * len(after),
            out_specs=[pl.BlockSpec((2 * SUB, FF), lambda i, place: (0, 0))] * 2,
        ),
        out_shape=[jax.ShapeDtypeStruct((2 * SUB, FF), BF)] * 2,
        compiler_params=params(),
        cost_estimate=WIDE_COSTS[step],
    )(place, *lefts, *rights, *after)


def down_kernel(place_ref, left_a, left_b, left_c, left_d, right_a, right_b, *refs):
    far_ref, near_ref = refs[-2:]
    for way, (a, b) in enumerate(((left_a, left_b), (left_c, left_d))):
        columns = slice(way * HALF, (way + 1) * HALF)
        total = jnp.dot(a[0], right_a[:, columns], preferred_element_type=F32)
        total = total + jnp.dot(b[0], right_b[:, columns], preferred_element_type=F32)
        near_ref[way] = total[:SUB].astype(BF)
        far_ref[way] = total[SUB:].astype(BF)


def down_parts(place, lefts, rights, after=()):
    up = pl.BlockSpec((1, 2 * SUB, ROWS), lambda i, place: (place[2 * i], 0, 0))
    down = pl.BlockSpec((1, 2 * SUB, ROWS), lambda i, place: (place[2 * i + 1], 0, 0))
    right = pl.BlockSpec((ROWS, FF), lambda i, place: (0, 0))
    return pl.pallas_call(
        down_kernel,
        grid_spec=pltpu.PrefetchScalarGridSpec(
            num_scalar_prefetch=1,
            grid=(NZ,),
            in_specs=[up, up, down, down, right, right]
            + [pl.BlockSpec(memory_space=pl.ANY)] * len(after),
            out_specs=[pl.BlockSpec((2, SUB, HALF), lambda i, place: (i, 0, 0))] * 2,
        ),
        out_shape=[jax.ShapeDtypeStruct((2 * NZ, SUB, HALF), BF)] * 2,
        compiler_params=params(),
        cost_estimate=PRODUCT,
    )(place, *lefts, *lefts, *rights, *after)


def around(up, down):
    return lax.ppermute(up, "dp", TO_UP), lax.ppermute(down, "dp", TO_DOWN)


def wide_add_kernel(part_up, part_down, up_ref, down_ref, *refs):
    refs[-2][...] = (part_up[...].astype(F32) + up_ref[...].astype(F32)).astype(BF)
    refs[-1][...] = (part_down[...].astype(F32) + down_ref[...].astype(F32)).astype(BF)


def wide_add(parts, moved, after=()):
    spec = pl.BlockSpec((SUB, FF), lambda i: (i, 0))
    return pl.pallas_call(
        wide_add_kernel,
        grid=(2,),
        in_specs=[spec] * 4 + [pl.BlockSpec(memory_space=pl.ANY)] * len(after),
        out_specs=[spec] * 2,
        out_shape=[jax.ShapeDtypeStruct((2 * SUB, FF), BF)] * 2,
        compiler_params=params(),
        cost_estimate=SHORT,
    )(*parts, *moved, *after)


def wide_last_kernel(part_up, part_down, up_ref, down_ref, *refs):
    mine_ref, away_ref = refs[-2:]
    sums = [
        (a[...].astype(F32) + b[...].astype(F32)).astype(BF)
        for a, b in ((part_up, up_ref), (part_down, down_ref))
    ]
    for step, out_ref in enumerate((away_ref, mine_ref)):

        @pl.when(pl.program_id(0) == step)
        def _():
            out_ref[0] = sums[0]
            out_ref[1] = sums[1]


def wide_last(parts, moved, after=()):
    spec = pl.BlockSpec((SUB, FF), lambda i: (1 - i, 0))
    out = pl.BlockSpec((2, SUB, FF), lambda i: (0, 0, 0))
    return pl.pallas_call(
        wide_last_kernel,
        grid=(2,),
        in_specs=[spec] * 4 + [pl.BlockSpec(memory_space=pl.ANY)] * len(after),
        out_specs=[out] * 2,
        out_shape=[jax.ShapeDtypeStruct((2, SUB, FF), BF)] * 2,
        compiler_params=params(),
        cost_estimate=SHORT,
    )(*parts, *moved, *after)


def down_add_kernel(moved, near_ref, far_ref, *refs):
    sums = [near_ref[k].astype(F32) + far_ref[k].astype(F32) for k in range(2)]
    if moved:
        sums = [a + ref[...].astype(F32) for a, ref in zip(sums, refs)]
    if len(refs[-1].shape) == 2 and refs[-1].shape[1] == FF:
        refs[-1][:, :HALF] = sums[0].astype(BF)
        refs[-1][:, HALF:] = sums[1].astype(BF)
    else:
        refs[-2][...] = sums[0].astype(BF)
        refs[-1][...] = sums[1].astype(BF)


def down_add(step, parts, moved=(), after=()):
    pair = pl.BlockSpec((2, SUB, HALF), lambda i: (step, 0, 0))
    one = pl.BlockSpec((SUB, HALF), lambda i: (0, 0))
    whole = pl.BlockSpec((SUB, FF), lambda i: (0, 0))
    last = step == NZ - 1
    return pl.pallas_call(
        functools.partial(down_add_kernel, len(moved) > 0),
        grid=(1,),
        in_specs=[pair] * 2
        + [one] * len(moved)
        + [pl.BlockSpec(memory_space=pl.ANY)] * len(after),
        out_specs=[whole] if last else [one] * 2,
        out_shape=[jax.ShapeDtypeStruct((SUB, FF), BF)]
        if last
        else [jax.ShapeDtypeStruct((SUB, HALF), BF)] * 2,
        compiler_params=params(),
        cost_estimate=LONG if step == 1 else SHORT,
    )(*parts, *moved, *after)


PLACES = np.array(
    [
        [v for s in range(NZ) for v in ((z - 1 - s) % NZ, (z + 1 + s) % NZ)] + [c, x]
        for z in range(NZ)
        for x in range(2)
        for c in range(2)
    ],
    np.int32,
)


def exchange(rows):
    width = rows.shape[1]
    out = lax.all_to_all(
        rows.reshape(EXPERTS, CAP, width), "expert", split_axis=0, concat_axis=0, tiled=True
    )
    return out.reshape(ROWS, width)


def local(tokens, grad_out, routes, probs, w_gate, w_up, w_down):
    place = lax.dynamic_slice(PLACES.reshape(-1), (10 * lax.axis_index("dp"),), (10,))
    gate, up, down = w_gate[0], w_up[0], w_down[0]
    picks, send_tokens = place_tokens(routes, tokens)
    row_tokens = exchange(send_tokens)
    send_grads = place_grads(picks, probs, grad_out)
    row_grads_in = exchange(send_grads)
    hidden, active, slope = forward(row_tokens, gate, up)
    lefts = turned(place, row_tokens, row_tokens, False, after=(hidden,))
    hiddens = (hidden, lax.ppermute(hidden, "dp", TO_CORE))
    both, wg = backward(
        row_grads_in, down, hidden, active, slope, after=(lefts[0], lefts[1], hiddens[1])
    )
    boths = (both, lax.ppermute(both, "dp", TO_CORE))
    dlefts = turned(place, row_grads_in, row_grads_in, True, after=(both,))
    ring0 = wide_parts(place, 0, lefts, boths, after=dlefts[:1])
    moved0 = around(*ring0)
    far, near = down_parts(place, dlefts, hiddens, after=ring0[:1])
    far_in = lax.ppermute(far, "dp", TO_X)
    parts1 = wide_parts(place, 1, lefts, boths, after=(far,))
    ring1 = wide_add(parts1, moved0)
    moved1 = around(*ring1)
    sent_rows = row_grads(both, gate, up, wg, after=ring1)
    returned = exchange(sent_rows)
    parts2 = wide_parts(place, 2, lefts, boths, after=(sent_rows,))
    down_pair = (near, far_in)
    down_ring0 = down_add(0, down_pair, after=parts2[:1])
    down_moved0 = around(*down_ring0)
    ring2 = wide_add(parts2, moved1, after=down_ring0)
    moved2 = around(*ring2)
    parts3 = wide_parts(place, 3, lefts, boths, after=ring2)
    down_ring1 = down_add(1, down_pair, down_moved0, after=parts3[:1])
    down_moved1 = around(*down_ring1)
    mine, away = wide_last(parts3, moved2, after=down_ring1)
    came = lax.ppermute(away, "dp", TO_X)
    down_ring2 = down_add(2, down_pair, down_moved1, after=(away,))
    down_moved2 = around(*down_ring2)
    grad_tokens, grad_weights = combine(picks, returned, after=down_ring2)
    (down_grad,) = down_add(3, down_pair, down_moved2, after=(grad_tokens,))
    mine, down_grad = lax.optimization_barrier((mine, down_grad))
    grad_gate = add(mine[0], came[0])[None]
    grad_up = add(mine[1], came[1])[None]
    grad_down = down_grad[None]
    return (grad_tokens, grad_weights.T, grad_gate, grad_up, grad_down)


def solution(mesh):
    spec = P(("dp", "expert"), None)
    weight = P("expert", None, None)
    out = P("expert", "dp", None)
    return jax.shard_map(
        local,
        mesh=mesh,
        in_specs=(spec, spec, spec, spec, weight, weight, weight),
        out_specs=(spec, spec, out, out, out),
        check_vma=False,
    )
```

```python
import functools

import jax
import jax.numpy as jnp
import numpy as np
from jax import lax
from jax.experimental import pallas as pl
from jax.experimental.pallas import tpu as pltpu
from jax.sharding import PartitionSpec as P

D = 3584
FF = 1024
TOP = 2
CAP = 64
EXPERTS = 8
ROWS = EXPERTS * CAP
TOK = 128
EXTRA = 128
WIDE = D + EXTRA
TILE = 1792
NT = D // TILE
NZ = 4
ZB = D // NZ
SUB = ZB // 4
HALF = FF // 2
BF = jnp.bfloat16
F32 = jnp.float32
FIRST = (((0,), (0,)), ((), ()))
LAST = (((1,), (1,)), ((), ()))
MB = 1 << 20


def params(limit=63):
    return pltpu.CompilerParams(vmem_limit_bytes=limit * MB)


def cost(flops, nbytes, trans=0):
    return pl.CostEstimate(flops=flops, bytes_accessed=nbytes, transcendentals=trans)


SHORT = cost(1, 1)
LONG = cost(40_000_000_000, 1)
PRODUCT = cost(16 * SUB * ROWS * FF, 8 * MB)
WIDE_COSTS = (PRODUCT, PRODUCT, cost(25_000_000_000, 1), SHORT)
SUMS = cost(10_000_000_000, 1)


def place_kernel(routes_ref, tokens_ref, picks_ref, out_ref):
    @pl.when(pl.program_id(0) == 0)
    def _():
        ids = lax.broadcasted_iota(jnp.int32, (EXPERTS, TOK), 0)
        named = [(routes_ref[k : k + 1, :] == ids).astype(F32) for k in range(TOP)]
        row = lax.broadcasted_iota(jnp.int32, (TOK, TOK), 0)
        col = lax.broadcasted_iota(jnp.int32, (TOK, TOK), 1)
        before = (row < col).astype(F32).astype(BF)
        rank = jnp.dot((named[0] + named[1]).astype(BF), before, preferred_element_type=F32)
        slot = lax.broadcasted_iota(jnp.int32, (CAP, TOK), 0).astype(F32)
        for k in range(TOP):
            for e in range(EXPERTS):
                hit = (slot == rank[e : e + 1, :]) & (named[k][e : e + 1, :] > 0.5)
                picks_ref[k, e * CAP : (e + 1) * CAP, :] = hit.astype(F32).astype(BF)

    both = picks_ref[0] + picks_ref[1]
    out_ref[...] = jnp.dot(both, tokens_ref[...], preferred_element_type=F32).astype(BF)


def place_tokens(routes, tokens):
    return pl.pallas_call(
        place_kernel,
        grid=(NT,),
        in_specs=[
            pl.BlockSpec((TOP, TOK), lambda i: (0, 0)),
            pl.BlockSpec((TOK, TILE), lambda i: (0, i)),
        ],
        out_specs=[
            pl.BlockSpec((TOP, ROWS, TOK), lambda i: (0, 0, 0)),
            pl.BlockSpec((ROWS, TILE), lambda i: (0, i)),
        ],
        out_shape=[
            jax.ShapeDtypeStruct((TOP, ROWS, TOK), BF),
            jax.ShapeDtypeStruct((ROWS, D), BF),
        ],
        compiler_params=params(),
        cost_estimate=cost(2 * ROWS * TOK * D, 5 * MB),
    )(routes.T, tokens)


def grads_kernel(picks_ref, probs_ref, grads_ref, out_ref):
    step = pl.program_id(0)

    @pl.when(step < NT)
    def _():
        both = picks_ref[0] + picks_ref[1]
        out_ref[...] = jnp.dot(both, grads_ref[...], preferred_element_type=F32).astype(BF)

    @pl.when(step == NT)
    def _():
        held = picks_ref[0] * probs_ref[0:1, :] + picks_ref[1] * probs_ref[1:2, :]
        ones = jnp.ones((TOK, EXTRA), BF)
        spread = jnp.dot(held, ones, preferred_element_type=F32)
        out_ref[:, :EXTRA] = spread.astype(BF)


def place_grads(picks, probs, grads):
    return pl.pallas_call(
        grads_kernel,
        grid=(NT + 1,),
        in_specs=[
            pl.BlockSpec((TOP, ROWS, TOK), lambda i: (0, 0, 0)),
            pl.BlockSpec((TOP, TOK), lambda i: (0, 0)),
            pl.BlockSpec((TOK, TILE), lambda i: (0, jnp.minimum(i, NT - 1))),
        ],
        out_specs=pl.BlockSpec((ROWS, TILE), lambda i: (0, i)),
        out_shape=jax.ShapeDtypeStruct((ROWS, WIDE), BF),
        compiler_params=params(),
        cost_estimate=cost(2 * ROWS * TOK * D, 5 * MB),
    )(picks, probs.T, grads)


def forward_kernel(x_ref, gate_ref, up_ref, hidden_ref, active_ref, slope_ref):
    x = x_ref[...]
    gate = jnp.dot(x, gate_ref[...], preferred_element_type=F32)
    up = jnp.dot(x, up_ref[...], preferred_element_type=F32)
    s = jax.nn.sigmoid(gate)
    active = gate * s
    hidden_ref[...] = (active * up).astype(BF)
    active_ref[...] = active
    slope_ref[...] = up * s * (1.0 + gate * (1.0 - s))


def forward(x, gate, up):
    n = 256
    return pl.pallas_call(
        forward_kernel,
        grid=(FF // n,),
        in_specs=[
            pl.BlockSpec((ROWS, D), lambda i: (0, 0)),
            pl.BlockSpec((D, n), lambda i: (0, i)),
            pl.BlockSpec((D, n), lambda i: (0, i)),
        ],
        out_specs=[pl.BlockSpec((ROWS, n), lambda i: (0, i))] * 3,
        out_shape=[
            jax.ShapeDtypeStruct((ROWS, FF), BF),
            jax.ShapeDtypeStruct((ROWS, FF), F32),
            jax.ShapeDtypeStruct((ROWS, FF), F32),
        ],
        compiler_params=params(),
        cost_estimate=cost(4 * ROWS * D * FF, 23 * MB, ROWS * FF),
    )(x, gate, up)


def backward_kernel(g_ref, down_ref, hidden_ref, active_ref, slope_ref, *refs):
    both_ref, wg_ref, total = refs[-3:]
    step = pl.program_id(0)
    back = jnp.dot(g_ref[:, :D], down_ref[...], preferred_element_type=F32)
    part = jnp.sum(back * hidden_ref[...].astype(F32), axis=1, keepdims=True)

    @pl.when(step == 0)
    def _():
        total[...] = jnp.zeros_like(total)

    total[...] += jnp.broadcast_to(part, total.shape)
    scaled = g_ref[:, D : D + 1].astype(F32) * back
    both_ref[0] = (scaled * slope_ref[...]).astype(BF)
    both_ref[1] = (scaled * active_ref[...]).astype(BF)
    wg_ref[...] = total[...].astype(BF)


def backward(g, down, hidden, active, slope, after=()):
    n = 512
    tile = pl.BlockSpec((ROWS, n), lambda i: (0, i))
    return pl.pallas_call(
        backward_kernel,
        grid=(FF // n,),
        in_specs=[
            pl.BlockSpec((ROWS, WIDE), lambda i: (0, 0)),
            pl.BlockSpec((D, n), lambda i: (0, i)),
            tile,
            tile,
            tile,
        ]
        + [pl.BlockSpec(memory_space=pl.ANY)] * len(after),
        out_specs=[
            pl.BlockSpec((2, ROWS, n), lambda i: (0, 0, i)),
            pl.BlockSpec((ROWS, EXTRA), lambda i: (0, 0)),
        ],
        out_shape=[
            jax.ShapeDtypeStruct((2, ROWS, FF), BF),
            jax.ShapeDtypeStruct((ROWS, EXTRA), BF),
        ],
        scratch_shapes=[pltpu.VMEM((ROWS, EXTRA), F32)],
        compiler_params=params(),
        cost_estimate=cost(2 * ROWS * D * FF, 18 * MB),
    )(g, down, hidden, active, slope, *after)


def rows_kernel(both_ref, gate_ref, up_ref, wg_ref, *refs):
    out_ref = refs[-1]
    step = pl.program_id(0)

    @pl.when(step < NT)
    def _():
        grad = lax.dot_general(both_ref[0], gate_ref[...], LAST, preferred_element_type=F32)
        grad = grad + lax.dot_general(both_ref[1], up_ref[...], LAST, preferred_element_type=F32)
        out_ref[...] = grad.astype(BF)

    @pl.when(step == NT)
    def _():
        out_ref[:, :EXTRA] = wg_ref[...]


def row_grads(both, gate, up, wg, after=()):
    clamp = lambda i: (jnp.minimum(i, NT - 1), 0)
    return pl.pallas_call(
        rows_kernel,
        grid=(NT + 1,),
        in_specs=[
            pl.BlockSpec((2, ROWS, FF), lambda i: (0, 0, 0)),
            pl.BlockSpec((TILE, FF), clamp),
            pl.BlockSpec((TILE, FF), clamp),
            pl.BlockSpec((ROWS, EXTRA), lambda i: (0, 0)),
        ]
        + [pl.BlockSpec(memory_space=pl.ANY)] * len(after),
        out_specs=pl.BlockSpec((ROWS, TILE), lambda i: (0, i)),
        out_shape=jax.ShapeDtypeStruct((ROWS, WIDE), BF),
        compiler_params=params(),
        cost_estimate=SHORT,
    )(both, gate, up, wg, *after)


def turned_kernel(scaled, deps, place_ref, x_ref, p_ref, *refs):
    send_ref, keep_ref, turned = refs[deps:]
    rows_in = x_ref[...]
    if scaled:
        rows_in = (p_ref[:, 0:1].astype(F32) * rows_in.astype(F32)).astype(BF)
    turned[...] = rows_in.T
    core, x = place_ref[8], place_ref[9]
    for j in range(2):
        rows = slice(j * SUB, (j + 1) * SUB)
        block = 2 * (x + j - 2 * x * j)
        far = pl.multiple_of((block + 1 - core) * SUB, SUB)
        near = pl.multiple_of((block + core) * SUB, SUB)
        send_ref[0, rows, :] = turned[pl.ds(far, SUB), :]
        keep_ref[0, rows, :] = turned[pl.ds(near, SUB), :]


def turned(place, x, p, scaled, after=()):
    last = (p.shape[1] // EXTRA) - 1
    send, keep = pl.pallas_call(
        functools.partial(turned_kernel, scaled, len(after)),
        grid_spec=pltpu.PrefetchScalarGridSpec(
            num_scalar_prefetch=1,
            grid=(NZ,),
            in_specs=[
                pl.BlockSpec((ROWS, ZB), lambda i, place: (0, i)),
                pl.BlockSpec((ROWS, EXTRA), lambda i, place: (0, last)),
            ]
            + [pl.BlockSpec(memory_space=pl.ANY)] * len(after),
            out_specs=[pl.BlockSpec((1, 2 * SUB, ROWS), lambda i, place: (i, 0, 0))] * 2,
            scratch_shapes=[pltpu.VMEM((ZB, ROWS), BF)],
        ),
        out_shape=[jax.ShapeDtypeStruct((NZ, 2 * SUB, ROWS), BF)] * 2,
        compiler_params=params(),
        cost_estimate=cost(ROWS * D, 8 * MB),
    )(place, x, p, *after)
    return keep, lax.ppermute(send, "dp", TO_CORE)


def combine_kernel(picks_ref, rows_ref, *refs):
    tokens_ref, weights_ref = refs[-2:]
    step = pl.program_id(0)

    @pl.when(step < NT)
    def _():
        both = picks_ref[0] + picks_ref[1]
        tokens_ref[...] = lax.dot_general(
            both, rows_ref[...], FIRST, preferred_element_type=F32
        ).astype(BF)

    @pl.when(step == NT)
    def _():
        for k in range(TOP):
            found = lax.dot_general(
                rows_ref[:, :EXTRA], picks_ref[k], FIRST, preferred_element_type=F32
            )
            weights_ref[k : k + 1, :] = found[0:1].astype(BF)


def combine(picks, rows, after=()):
    return pl.pallas_call(
        combine_kernel,
        grid=(NT + 1,),
        in_specs=[
            pl.BlockSpec((TOP, ROWS, TOK), lambda i: (0, 0, 0)),
            pl.BlockSpec((ROWS, TILE), lambda i: (0, i)),
        ]
        + [pl.BlockSpec(memory_space=pl.ANY)] * len(after),
        out_specs=[
            pl.BlockSpec((TOK, TILE), lambda i: (0, jnp.minimum(i, NT - 1))),
            pl.BlockSpec((TOP, TOK), lambda i: (0, 0)),
        ],
        out_shape=[
            jax.ShapeDtypeStruct((TOK, D), BF),
            jax.ShapeDtypeStruct((TOP, TOK), BF),
        ],
        compiler_params=params(),
        cost_estimate=SHORT,
    )(picks, rows, *after)


def moves(f):
    pairs = []
    for z in range(NZ):
        for x in range(2):
            for c in range(2):
                tz, tx, tc = f(z, x, c)
                pairs.append((z * 4 + x * 2 + c, (tz % NZ) * 4 + tx * 2 + tc))
    return pairs


TO_CORE = moves(lambda z, x, c: (z, x, 1 - c))
TO_UP = moves(lambda z, x, c: (z + 1, x, c))
TO_DOWN = moves(lambda z, x, c: (z - 1, x, c))
TO_TWO = moves(lambda z, x, c: (z + 2, x, c))
TO_X = moves(lambda z, x, c: (z, 1 - x, c))


def add(*parts):
    total = parts[0].astype(F32)
    for part in parts[1:]:
        total = total + part.astype(F32)
    return total.astype(BF)


def wide_kernel(place_ref, left_a, left_b, right_a, right_b, *refs):
    total = jnp.dot(left_a[0], right_a[0], preferred_element_type=F32)
    total = total + jnp.dot(left_b[0], right_b[0], preferred_element_type=F32)
    for k, out_ref in enumerate(refs[-2:]):

        @pl.when(pl.program_id(0) == k)
        def _():
            out_ref[...] = total.astype(BF)


def wide_parts(place, step, lefts, rights, after=()):
    left = pl.BlockSpec((1, 2 * SUB, ROWS), lambda i, place: (place[2 * step + i], 0, 0))
    right = pl.BlockSpec((1, ROWS, FF), lambda i, place: (i, 0, 0))
    return pl.pallas_call(
        wide_kernel,
        grid_spec=pltpu.PrefetchScalarGridSpec(
            num_scalar_prefetch=1,
            grid=(2,),
            in_specs=[left, left, right, right]
            + [pl.BlockSpec(memory_space=pl.ANY)] * len(after),
            out_specs=[pl.BlockSpec((2 * SUB, FF), lambda i, place: (0, 0))] * 2,
        ),
        out_shape=[jax.ShapeDtypeStruct((2 * SUB, FF), BF)] * 2,
        compiler_params=params(),
        cost_estimate=WIDE_COSTS[step],
    )(place, *lefts, *rights, *after)


def down_kernel(place_ref, left_a, left_b, right_a, right_b, *refs):
    far_ref, near_ref = refs[-2:]
    total = jnp.dot(left_a[0], right_a[...], preferred_element_type=F32)
    total = total + jnp.dot(left_b[0], right_b[...], preferred_element_type=F32)
    near_ref[0] = total[:SUB].astype(BF)
    far_ref[0] = total[SUB:].astype(BF)


def down_parts(place, lefts, rights, after=()):
    left = pl.BlockSpec((1, 2 * SUB, ROWS), lambda i, place: (place[i + 3 * (i // 3)], 0, 0))
    right = pl.BlockSpec((ROWS, FF), lambda i, place: (0, 0))
    return pl.pallas_call(
        down_kernel,
        grid_spec=pltpu.PrefetchScalarGridSpec(
            num_scalar_prefetch=1,
            grid=(NZ,),
            in_specs=[left, left, right, right]
            + [pl.BlockSpec(memory_space=pl.ANY)] * len(after),
            out_specs=[pl.BlockSpec((1, SUB, FF), lambda i, place: (i, 0, 0))] * 2,
        ),
        out_shape=[jax.ShapeDtypeStruct((NZ, SUB, FF), BF)] * 2,
        compiler_params=params(),
        cost_estimate=PRODUCT,
    )(place, *lefts, *rights, *after)


def around(up, down):
    return lax.ppermute(up, "dp", TO_UP), lax.ppermute(down, "dp", TO_DOWN)


def wide_add_kernel(part_up, part_down, up_ref, down_ref, *refs):
    refs[-2][...] = (part_up[...].astype(F32) + up_ref[...].astype(F32)).astype(BF)
    refs[-1][...] = (part_down[...].astype(F32) + down_ref[...].astype(F32)).astype(BF)


def wide_add(parts, moved, after=()):
    spec = pl.BlockSpec((SUB, FF), lambda i: (i, 0))
    return pl.pallas_call(
        wide_add_kernel,
        grid=(2,),
        in_specs=[spec] * 4 + [pl.BlockSpec(memory_space=pl.ANY)] * len(after),
        out_specs=[spec] * 2,
        out_shape=[jax.ShapeDtypeStruct((2 * SUB, FF), BF)] * 2,
        compiler_params=params(),
        cost_estimate=SHORT,
    )(*parts, *moved, *after)


def wide_last_kernel(part_up, part_down, up_ref, down_ref, *refs):
    mine_ref, away_ref = refs[-2:]
    sums = [
        (a[...].astype(F32) + b[...].astype(F32)).astype(BF)
        for a, b in ((part_up, up_ref), (part_down, down_ref))
    ]
    for step, out_ref in enumerate((away_ref, mine_ref)):

        @pl.when(pl.program_id(0) == step)
        def _():
            out_ref[0] = sums[0]
            out_ref[1] = sums[1]


def wide_last(parts, moved, after=()):
    spec = pl.BlockSpec((SUB, FF), lambda i: (1 - i, 0))
    out = pl.BlockSpec((2, SUB, FF), lambda i: (0, 0, 0))
    return pl.pallas_call(
        wide_last_kernel,
        grid=(2,),
        in_specs=[spec] * 4 + [pl.BlockSpec(memory_space=pl.ANY)] * len(after),
        out_specs=[out] * 2,
        out_shape=[jax.ShapeDtypeStruct((2, SUB, FF), BF)] * 2,
        compiler_params=params(),
        cost_estimate=SHORT,
    )(*parts, *moved, *after)


def down_sums_kernel(near_ref, far_ref, *refs):
    for k, out_ref in enumerate(refs[-3:]):
        out_ref[...] = (near_ref[k].astype(F32) + far_ref[k].astype(F32)).astype(BF)


def down_sums(near, far, after=()):
    some = pl.BlockSpec((NZ - 1, SUB, FF), lambda i: (0, 0, 0))
    return pl.pallas_call(
        down_sums_kernel,
        grid=(1,),
        in_specs=[some] * 2 + [pl.BlockSpec(memory_space=pl.ANY)] * len(after),
        out_specs=[pl.BlockSpec((SUB, FF), lambda i: (0, 0))] * 3,
        out_shape=[jax.ShapeDtypeStruct((SUB, FF), BF)] * 3,
        compiler_params=params(),
        cost_estimate=SUMS,
    )(near, far, *after)


def down_last_kernel(near_ref, far_ref, a_ref, b_ref, c_ref, *refs):
    total = near_ref[0].astype(F32) + far_ref[0].astype(F32)
    for ref in (a_ref, b_ref, c_ref):
        total = total + ref[...].astype(F32)
    refs[-1][...] = total.astype(BF)


def down_last(near, far, came, after=()):
    half = SUB // 2
    own = pl.BlockSpec((1, half, FF), lambda i: (NZ - 1, i, 0))
    spec = pl.BlockSpec((half, FF), lambda i: (i, 0))
    return pl.pallas_call(
        down_last_kernel,
        grid=(2,),
        in_specs=[own] * 2 + [spec] * 3 + [pl.BlockSpec(memory_space=pl.ANY)] * len(after),
        out_specs=spec,
        out_shape=jax.ShapeDtypeStruct((SUB, FF), BF),
        compiler_params=params(),
        cost_estimate=LONG,
    )(near, far, *came, *after)


PLACES = np.array(
    [
        [v for s in range(NZ) for v in ((z - 1 - s) % NZ, (z + 1 + s) % NZ)] + [c, x]
        for z in range(NZ)
        for x in range(2)
        for c in range(2)
    ],
    np.int32,
)


def exchange(rows):
    width = rows.shape[1]
    out = lax.all_to_all(
        rows.reshape(EXPERTS, CAP, width), "expert", split_axis=0, concat_axis=0, tiled=True
    )
    return out.reshape(ROWS, width)


def local(tokens, grad_out, routes, probs, w_gate, w_up, w_down):
    place = lax.dynamic_slice(PLACES.reshape(-1), (10 * lax.axis_index("dp"),), (10,))
    gate, up, down = w_gate[0], w_up[0], w_down[0]
    picks, send_tokens = place_tokens(routes, tokens)
    row_tokens = exchange(send_tokens)
    send_grads = place_grads(picks, probs, grad_out)
    row_grads_in = exchange(send_grads)
    hidden, active, slope = forward(row_tokens, gate, up)
    lefts = turned(place, row_tokens, row_tokens, False, after=(hidden,))
    hiddens = (hidden, lax.ppermute(hidden, "dp", TO_CORE))
    both, wg = backward(
        row_grads_in, down, hidden, active, slope, after=(lefts[0], lefts[1], hiddens[1])
    )
    boths = (both, lax.ppermute(both, "dp", TO_CORE))
    dlefts = turned(place, row_grads_in, row_grads_in, True, after=(both,))
    ring0 = wide_parts(place, 0, lefts, boths, after=dlefts[:1])
    moved0 = around(*ring0)
    far, near = down_parts(place, dlefts, hiddens, after=ring0[:1])
    far_in = lax.ppermute(far, "dp", TO_X)
    parts1 = wide_parts(place, 1, lefts, boths, after=(far,))
    ring1 = wide_add(parts1, moved0)
    moved1 = around(*ring1)
    sent_rows = row_grads(both, gate, up, wg, after=ring1)
    returned = exchange(sent_rows)
    parts2 = wide_parts(place, 2, lefts, boths, after=(sent_rows,))
    ring2 = wide_add(parts2, moved1)
    moved2 = around(*ring2)
    sums = down_sums(near, far_in, after=ring2)
    ways = (TO_DOWN, TO_UP, TO_TWO)
    down_came = [lax.ppermute(part, "dp", way) for part, way in zip(sums, ways)]
    parts3 = wide_parts(place, 3, lefts, boths, after=sums)
    mine, away = wide_last(parts3, moved2)
    came = lax.ppermute(away, "dp", TO_X)
    grad_tokens, grad_weights = combine(picks, returned, after=(away,))
    down_grad = down_last(near, far_in, down_came, after=(grad_tokens,))
    mine, down_grad = lax.optimization_barrier((mine, down_grad))
    grad_gate = add(mine[0], came[0])[None]
    grad_up = add(mine[1], came[1])[None]
    grad_down = down_grad[None]
    return (grad_tokens, grad_weights.T, grad_gate, grad_up, grad_down)


def solution(mesh):
    spec = P(("dp", "expert"), None)
    weight = P("expert", None, None)
    out = P("expert", "dp", None)
    return jax.shard_map(
        local,
        mesh=mesh,
        in_specs=(spec, spec, spec, spec, weight, weight, weight),
        out_specs=(spec, spec, out, out, out),
        check_vma=False,
    )
```

```python
import functools

import jax
import jax.numpy as jnp
import numpy as np
from jax import lax
from jax.experimental import pallas as pl
from jax.experimental.pallas import tpu as pltpu
from jax.sharding import PartitionSpec as P

D = 3584
FF = 1024
TOP = 2
CAP = 64
EXPERTS = 8
ROWS = EXPERTS * CAP
TOK = 128
EXTRA = 128
WIDE = D + EXTRA
TILE = 1792
NT = D // TILE
NZ = 4
ZB = D // NZ
SUB = ZB // 4
HALF = FF // 2
BF = jnp.bfloat16
F32 = jnp.float32
FIRST = (((0,), (0,)), ((), ()))
LAST = (((1,), (1,)), ((), ()))
MB = 1 << 20


def params(limit=63):
    return pltpu.CompilerParams(vmem_limit_bytes=limit * MB + MB // 2)


def cost(flops, nbytes, trans=0):
    return pl.CostEstimate(flops=flops, bytes_accessed=nbytes, transcendentals=trans)


SHORT = cost(1, 1)
LONG = cost(40_000_000_000, 1)
PRODUCT = cost(16 * SUB * ROWS * FF, 8 * MB)
WIDE_COSTS = (PRODUCT, PRODUCT, cost(25_000_000_000, 1), SHORT)
SUMS = cost(10_000_000_000, 1)


def place_kernel(routes_ref, tokens_ref, picks_ref, out_ref):
    @pl.when(pl.program_id(0) == 0)
    def _():
        ids = lax.broadcasted_iota(jnp.int32, (EXPERTS, TOK), 0)
        named = [(routes_ref[k : k + 1, :] == ids).astype(F32) for k in range(TOP)]
        row = lax.broadcasted_iota(jnp.int32, (TOK, TOK), 0)
        col = lax.broadcasted_iota(jnp.int32, (TOK, TOK), 1)
        before = (row < col).astype(F32).astype(BF)
        rank = jnp.dot((named[0] + named[1]).astype(BF), before, preferred_element_type=F32)
        slot = lax.broadcasted_iota(jnp.int32, (CAP, TOK), 0).astype(F32)
        for k in range(TOP):
            for e in range(EXPERTS):
                hit = (slot == rank[e : e + 1, :]) & (named[k][e : e + 1, :] > 0.5)
                picks_ref[k, e * CAP : (e + 1) * CAP, :] = hit.astype(F32).astype(BF)

    both = picks_ref[0] + picks_ref[1]
    out_ref[...] = jnp.dot(both, tokens_ref[...], preferred_element_type=F32).astype(BF)


def place_tokens(routes, tokens):
    return pl.pallas_call(
        place_kernel,
        grid=(NT,),
        in_specs=[
            pl.BlockSpec((TOP, TOK), lambda i: (0, 0)),
            pl.BlockSpec((TOK, TILE), lambda i: (0, i)),
        ],
        out_specs=[
            pl.BlockSpec((TOP, ROWS, TOK), lambda i: (0, 0, 0)),
            pl.BlockSpec((ROWS, TILE), lambda i: (0, i)),
        ],
        out_shape=[
            jax.ShapeDtypeStruct((TOP, ROWS, TOK), BF),
            jax.ShapeDtypeStruct((ROWS, D), BF),
        ],
        compiler_params=params(),
        cost_estimate=cost(2 * ROWS * TOK * D, 5 * MB),
    )(routes.T, tokens)


def grads_kernel(picks_ref, probs_ref, grads_ref, out_ref):
    step = pl.program_id(0)

    @pl.when(step < NT)
    def _():
        both = picks_ref[0] + picks_ref[1]
        out_ref[...] = jnp.dot(both, grads_ref[...], preferred_element_type=F32).astype(BF)

    @pl.when(step == NT)
    def _():
        held = picks_ref[0] * probs_ref[0:1, :] + picks_ref[1] * probs_ref[1:2, :]
        ones = jnp.ones((TOK, EXTRA), BF)
        spread = jnp.dot(held, ones, preferred_element_type=F32)
        out_ref[:, :EXTRA] = spread.astype(BF)


def place_grads(picks, probs, grads):
    return pl.pallas_call(
        grads_kernel,
        grid=(NT + 1,),
        in_specs=[
            pl.BlockSpec((TOP, ROWS, TOK), lambda i: (0, 0, 0)),
            pl.BlockSpec((TOP, TOK), lambda i: (0, 0)),
            pl.BlockSpec((TOK, TILE), lambda i: (0, jnp.minimum(i, NT - 1))),
        ],
        out_specs=pl.BlockSpec((ROWS, TILE), lambda i: (0, i)),
        out_shape=jax.ShapeDtypeStruct((ROWS, WIDE), BF),
        compiler_params=params(),
        cost_estimate=cost(2 * ROWS * TOK * D, 5 * MB),
    )(picks, probs.T, grads)


def forward_kernel(x_ref, gate_ref, up_ref, hidden_ref, active_ref, slope_ref):
    x = x_ref[...]
    gate = jnp.dot(x, gate_ref[...], preferred_element_type=F32)
    up = jnp.dot(x, up_ref[...], preferred_element_type=F32)
    s = jax.nn.sigmoid(gate)
    active = gate * s
    hidden_ref[...] = (active * up).astype(BF)
    active_ref[...] = active
    slope_ref[...] = up * s * (1.0 + gate * (1.0 - s))


def forward(x, gate, up):
    n = 256
    return pl.pallas_call(
        forward_kernel,
        grid=(FF // n,),
        in_specs=[
            pl.BlockSpec((ROWS, D), lambda i: (0, 0)),
            pl.BlockSpec((D, n), lambda i: (0, i)),
            pl.BlockSpec((D, n), lambda i: (0, i)),
        ],
        out_specs=[pl.BlockSpec((ROWS, n), lambda i: (0, i))] * 3,
        out_shape=[
            jax.ShapeDtypeStruct((ROWS, FF), BF),
            jax.ShapeDtypeStruct((ROWS, FF), F32),
            jax.ShapeDtypeStruct((ROWS, FF), F32),
        ],
        compiler_params=params(),
        cost_estimate=cost(4 * ROWS * D * FF, 23 * MB, ROWS * FF),
    )(x, gate, up)


def backward_kernel(g_ref, down_ref, hidden_ref, active_ref, slope_ref, *refs):
    both_ref, wg_ref, total = refs[-3:]
    step = pl.program_id(0)
    back = jnp.dot(g_ref[:, :D], down_ref[...], preferred_element_type=F32)
    part = jnp.sum(back * hidden_ref[...].astype(F32), axis=1, keepdims=True)

    @pl.when(step == 0)
    def _():
        total[...] = jnp.zeros_like(total)

    total[...] += jnp.broadcast_to(part, total.shape)
    scaled = g_ref[:, D : D + 1].astype(F32) * back
    both_ref[0] = (scaled * slope_ref[...]).astype(BF)
    both_ref[1] = (scaled * active_ref[...]).astype(BF)
    wg_ref[...] = total[...].astype(BF)


def backward(g, down, hidden, active, slope, after=()):
    n = 512
    tile = pl.BlockSpec((ROWS, n), lambda i: (0, i))
    return pl.pallas_call(
        backward_kernel,
        grid=(FF // n,),
        in_specs=[
            pl.BlockSpec((ROWS, WIDE), lambda i: (0, 0)),
            pl.BlockSpec((D, n), lambda i: (0, i)),
            tile,
            tile,
            tile,
        ]
        + [pl.BlockSpec(memory_space=pl.ANY)] * len(after),
        out_specs=[
            pl.BlockSpec((2, ROWS, n), lambda i: (0, 0, i)),
            pl.BlockSpec((ROWS, EXTRA), lambda i: (0, 0)),
        ],
        out_shape=[
            jax.ShapeDtypeStruct((2, ROWS, FF), BF),
            jax.ShapeDtypeStruct((ROWS, EXTRA), BF),
        ],
        scratch_shapes=[pltpu.VMEM((ROWS, EXTRA), F32)],
        compiler_params=params(),
        cost_estimate=cost(2 * ROWS * D * FF, 18 * MB),
    )(g, down, hidden, active, slope, *after)


def rows_kernel(both_ref, gate_ref, up_ref, wg_ref, *refs):
    out_ref = refs[-1]
    step = pl.program_id(0)

    @pl.when(step < NT)
    def _():
        grad = lax.dot_general(both_ref[0], gate_ref[...], LAST, preferred_element_type=F32)
        grad = grad + lax.dot_general(both_ref[1], up_ref[...], LAST, preferred_element_type=F32)
        out_ref[...] = grad.astype(BF)

    @pl.when(step == NT)
    def _():
        out_ref[:, :EXTRA] = wg_ref[...]


def row_grads(both, gate, up, wg, after=()):
    clamp = lambda i: (jnp.minimum(i, NT - 1), 0)
    return pl.pallas_call(
        rows_kernel,
        grid=(NT + 1,),
        in_specs=[
            pl.BlockSpec((2, ROWS, FF), lambda i: (0, 0, 0)),
            pl.BlockSpec((TILE, FF), clamp),
            pl.BlockSpec((TILE, FF), clamp),
            pl.BlockSpec((ROWS, EXTRA), lambda i: (0, 0)),
        ]
        + [pl.BlockSpec(memory_space=pl.ANY)] * len(after),
        out_specs=pl.BlockSpec((ROWS, TILE), lambda i: (0, i)),
        out_shape=jax.ShapeDtypeStruct((ROWS, WIDE), BF),
        compiler_params=params(),
        cost_estimate=SHORT,
    )(both, gate, up, wg, *after)


def turned_kernel(scaled, deps, place_ref, x_ref, p_ref, *refs):
    send_ref, keep_ref, turned = refs[deps:]
    rows_in = x_ref[...]
    if scaled:
        rows_in = (p_ref[:, 0:1].astype(F32) * rows_in.astype(F32)).astype(BF)
    turned[...] = rows_in.T
    core, x = place_ref[8], place_ref[9]
    for j in range(2):
        rows = slice(j * SUB, (j + 1) * SUB)
        block = 2 * (x + j - 2 * x * j)
        far = pl.multiple_of((block + 1 - core) * SUB, SUB)
        near = pl.multiple_of((block + core) * SUB, SUB)
        send_ref[0, rows, :] = turned[pl.ds(far, SUB), :]
        keep_ref[0, rows, :] = turned[pl.ds(near, SUB), :]


def turned(place, x, p, scaled, after=()):
    last = (p.shape[1] // EXTRA) - 1
    send, keep = pl.pallas_call(
        functools.partial(turned_kernel, scaled, len(after)),
        grid_spec=pltpu.PrefetchScalarGridSpec(
            num_scalar_prefetch=1,
            grid=(NZ,),
            in_specs=[
                pl.BlockSpec((ROWS, ZB), lambda i, place: (0, i)),
                pl.BlockSpec((ROWS, EXTRA), lambda i, place: (0, last)),
            ]
            + [pl.BlockSpec(memory_space=pl.ANY)] * len(after),
            out_specs=[pl.BlockSpec((1, 2 * SUB, ROWS), lambda i, place: (i, 0, 0))] * 2,
            scratch_shapes=[pltpu.VMEM((ZB, ROWS), BF)],
        ),
        out_shape=[jax.ShapeDtypeStruct((NZ, 2 * SUB, ROWS), BF)] * 2,
        compiler_params=params(),
        cost_estimate=cost(ROWS * D, 8 * MB),
    )(place, x, p, *after)
    return keep, lax.ppermute(send, "dp", TO_CORE)


def combine_kernel(picks_ref, rows_ref, *refs):
    tokens_ref, weights_ref = refs[-2:]
    step = pl.program_id(0)

    @pl.when(step < NT)
    def _():
        both = picks_ref[0] + picks_ref[1]
        tokens_ref[...] = lax.dot_general(
            both, rows_ref[...], FIRST, preferred_element_type=F32
        ).astype(BF)

    @pl.when(step == NT)
    def _():
        for k in range(TOP):
            found = lax.dot_general(
                rows_ref[:, :EXTRA], picks_ref[k], FIRST, preferred_element_type=F32
            )
            weights_ref[k : k + 1, :] = found[0:1].astype(BF)


def combine(picks, rows, after=()):
    return pl.pallas_call(
        combine_kernel,
        grid=(NT + 1,),
        in_specs=[
            pl.BlockSpec((TOP, ROWS, TOK), lambda i: (0, 0, 0)),
            pl.BlockSpec((ROWS, TILE), lambda i: (0, i)),
        ]
        + [pl.BlockSpec(memory_space=pl.ANY)] * len(after),
        out_specs=[
            pl.BlockSpec((TOK, TILE), lambda i: (0, jnp.minimum(i, NT - 1))),
            pl.BlockSpec((TOP, TOK), lambda i: (0, 0)),
        ],
        out_shape=[
            jax.ShapeDtypeStruct((TOK, D), BF),
            jax.ShapeDtypeStruct((TOP, TOK), BF),
        ],
        compiler_params=params(),
        cost_estimate=SHORT,
    )(picks, rows, *after)


def moves(f):
    pairs = []
    for z in range(NZ):
        for x in range(2):
            for c in range(2):
                tz, tx, tc = f(z, x, c)
                pairs.append((z * 4 + x * 2 + c, (tz % NZ) * 4 + tx * 2 + tc))
    return pairs


TO_CORE = moves(lambda z, x, c: (z, x, 1 - c))
TO_UP = moves(lambda z, x, c: (z + 1, x, c))
TO_DOWN = moves(lambda z, x, c: (z - 1, x, c))
TO_TWO = moves(lambda z, x, c: (z + 2, x, c))
TO_X = moves(lambda z, x, c: (z, 1 - x, c))


def add(*parts):
    total = parts[0].astype(F32)
    for part in parts[1:]:
        total = total + part.astype(F32)
    return total.astype(BF)


def wide_kernel(place_ref, left_a, left_b, right_a, right_b, *refs):
    total = jnp.dot(left_a[0], right_a[0], preferred_element_type=F32)
    total = total + jnp.dot(left_b[0], right_b[0], preferred_element_type=F32)
    for k, out_ref in enumerate(refs[-2:]):

        @pl.when(pl.program_id(0) == k)
        def _():
            out_ref[...] = total.astype(BF)


def wide_parts(place, step, lefts, rights, after=()):
    left = pl.BlockSpec((1, 2 * SUB, ROWS), lambda i, place: (place[2 * step + i], 0, 0))
    right = pl.BlockSpec((1, ROWS, FF), lambda i, place: (i, 0, 0))
    return pl.pallas_call(
        wide_kernel,
        grid_spec=pltpu.PrefetchScalarGridSpec(
            num_scalar_prefetch=1,
            grid=(2,),
            in_specs=[left, left, right, right]
            + [pl.BlockSpec(memory_space=pl.ANY)] * len(after),
            out_specs=[pl.BlockSpec((2 * SUB, FF), lambda i, place: (0, 0))] * 2,
        ),
        out_shape=[jax.ShapeDtypeStruct((2 * SUB, FF), BF)] * 2,
        compiler_params=params(),
        cost_estimate=WIDE_COSTS[step],
    )(place, *lefts, *rights, *after)


def down_kernel(place_ref, left_a, left_b, right_a, right_b, *refs):
    far_ref, near_ref = refs[-2:]
    total = jnp.dot(left_a[0], right_a[...], preferred_element_type=F32)
    total = total + jnp.dot(left_b[0], right_b[...], preferred_element_type=F32)
    near_ref[0] = total[:SUB].astype(BF)
    far_ref[0] = total[SUB:].astype(BF)


def down_parts(place, lefts, rights, after=()):
    left = pl.BlockSpec((1, 2 * SUB, ROWS), lambda i, place: (place[i + 3 * (i // 3)], 0, 0))
    right = pl.BlockSpec((ROWS, FF), lambda i, place: (0, 0))
    return pl.pallas_call(
        down_kernel,
        grid_spec=pltpu.PrefetchScalarGridSpec(
            num_scalar_prefetch=1,
            grid=(NZ,),
            in_specs=[left, left, right, right]
            + [pl.BlockSpec(memory_space=pl.ANY)] * len(after),
            out_specs=[pl.BlockSpec((1, SUB, FF), lambda i, place: (i, 0, 0))] * 2,
        ),
        out_shape=[jax.ShapeDtypeStruct((NZ, SUB, FF), BF)] * 2,
        compiler_params=params(),
        cost_estimate=PRODUCT,
    )(place, *lefts, *rights, *after)


def around(up, down):
    return lax.ppermute(up, "dp", TO_UP), lax.ppermute(down, "dp", TO_DOWN)


def wide_add_kernel(part_up, part_down, up_ref, down_ref, *refs):
    refs[-2][...] = (part_up[...].astype(F32) + up_ref[...].astype(F32)).astype(BF)
    refs[-1][...] = (part_down[...].astype(F32) + down_ref[...].astype(F32)).astype(BF)


def wide_add(parts, moved, after=()):
    spec = pl.BlockSpec((SUB, FF), lambda i: (i, 0))
    return pl.pallas_call(
        wide_add_kernel,
        grid=(2,),
        in_specs=[spec] * 4 + [pl.BlockSpec(memory_space=pl.ANY)] * len(after),
        out_specs=[spec] * 2,
        out_shape=[jax.ShapeDtypeStruct((2 * SUB, FF), BF)] * 2,
        compiler_params=params(),
        cost_estimate=SHORT,
    )(*parts, *moved, *after)


def wide_last_kernel(part_up, part_down, up_ref, down_ref, *refs):
    mine_ref, away_ref = refs[-2:]
    sums = [
        (a[...].astype(F32) + b[...].astype(F32)).astype(BF)
        for a, b in ((part_up, up_ref), (part_down, down_ref))
    ]
    for step, out_ref in enumerate((away_ref, mine_ref)):

        @pl.when(pl.program_id(0) == step)
        def _():
            out_ref[0] = sums[0]
            out_ref[1] = sums[1]


def wide_last(parts, moved, after=()):
    spec = pl.BlockSpec((SUB, FF), lambda i: (1 - i, 0))
    out = pl.BlockSpec((2, SUB, FF), lambda i: (0, 0, 0))
    return pl.pallas_call(
        wide_last_kernel,
        grid=(2,),
        in_specs=[spec] * 4 + [pl.BlockSpec(memory_space=pl.ANY)] * len(after),
        out_specs=[out] * 2,
        out_shape=[jax.ShapeDtypeStruct((2, SUB, FF), BF)] * 2,
        compiler_params=params(),
        cost_estimate=SHORT,
    )(*parts, *moved, *after)


def down_sums_kernel(near_ref, far_ref, *refs):
    for k, out_ref in enumerate(refs[-3:]):
        out_ref[...] = (near_ref[k].astype(F32) + far_ref[k].astype(F32)).astype(BF)


def down_sums(near, far, after=()):
    some = pl.BlockSpec((NZ - 1, SUB, FF), lambda i: (0, 0, 0))
    return pl.pallas_call(
        down_sums_kernel,
        grid=(1,),
        in_specs=[some] * 2 + [pl.BlockSpec(memory_space=pl.ANY)] * len(after),
        out_specs=[pl.BlockSpec((SUB, FF), lambda i: (0, 0))] * 3,
        out_shape=[jax.ShapeDtypeStruct((SUB, FF), BF)] * 3,
        compiler_params=params(),
        cost_estimate=SUMS,
    )(near, far, *after)


def down_last_kernel(near_ref, far_ref, a_ref, b_ref, c_ref, *refs):
    total = near_ref[0].astype(F32) + far_ref[0].astype(F32)
    for ref in (a_ref, b_ref, c_ref):
        total = total + ref[...].astype(F32)
    refs[-1][...] = total.astype(BF)


def down_last(near, far, came, after=()):
    half = SUB // 2
    own = pl.BlockSpec((1, half, FF), lambda i: (NZ - 1, i, 0))
    spec = pl.BlockSpec((half, FF), lambda i: (i, 0))
    return pl.pallas_call(
        down_last_kernel,
        grid=(2,),
        in_specs=[own] * 2 + [spec] * 3 + [pl.BlockSpec(memory_space=pl.ANY)] * len(after),
        out_specs=spec,
        out_shape=jax.ShapeDtypeStruct((SUB, FF), BF),
        compiler_params=params(),
        cost_estimate=LONG,
    )(near, far, *came, *after)


PLACES = np.array(
    [
        [v for s in range(NZ) for v in ((z - 1 - s) % NZ, (z + 1 + s) % NZ)] + [c, x]
        for z in range(NZ)
        for x in range(2)
        for c in range(2)
    ],
    np.int32,
)


def exchange(rows):
    width = rows.shape[1]
    out = lax.all_to_all(
        rows.reshape(EXPERTS, CAP, width), "expert", split_axis=0, concat_axis=0, tiled=True
    )
    return out.reshape(ROWS, width)


def local(tokens, grad_out, routes, probs, w_gate, w_up, w_down):
    place = lax.dynamic_slice(PLACES.reshape(-1), (10 * lax.axis_index("dp"),), (10,))
    gate, up, down = w_gate[0], w_up[0], w_down[0]
    picks, send_tokens = place_tokens(routes, tokens)
    row_tokens = exchange(send_tokens)
    send_grads = place_grads(picks, probs, grad_out)
    row_grads_in = exchange(send_grads)
    hidden, active, slope = forward(row_tokens, gate, up)
    lefts = turned(place, row_tokens, row_tokens, False, after=(hidden,))
    hiddens = (hidden, lax.ppermute(hidden, "dp", TO_CORE))
    both, wg = backward(
        row_grads_in, down, hidden, active, slope, after=(lefts[0], lefts[1], hiddens[1])
    )
    boths = (both, lax.ppermute(both, "dp", TO_CORE))
    dlefts = turned(place, row_grads_in, row_grads_in, True, after=(both,))
    ring0 = wide_parts(place, 0, lefts, boths, after=dlefts[:1])
    moved0 = around(*ring0)
    far, near = down_parts(place, dlefts, hiddens, after=ring0[:1])
    far_in = lax.ppermute(far, "dp", TO_X)
    parts1 = wide_parts(place, 1, lefts, boths, after=(far,))
    ring1 = wide_add(parts1, moved0)
    moved1 = around(*ring1)
    sent_rows = row_grads(both, gate, up, wg, after=ring1)
    returned = exchange(sent_rows)
    parts2 = wide_parts(place, 2, lefts, boths, after=(sent_rows,))
    ring2 = wide_add(parts2, moved1)
    moved2 = around(*ring2)
    parts3 = wide_parts(place, 3, lefts, boths, after=ring2)
    sums = down_sums(near, far_in, after=parts3)
    ways = (TO_DOWN, TO_UP, TO_TWO)
    down_came = [lax.ppermute(part, "dp", way) for part, way in zip(sums, ways)]
    mine, away = wide_last(parts3, moved2, after=sums)
    came = lax.ppermute(away, "dp", TO_X)
    grad_tokens, grad_weights = combine(picks, returned, after=(away,))
    down_grad = down_last(near, far_in, down_came, after=(grad_tokens,))
    mine, down_grad = lax.optimization_barrier((mine, down_grad))
    grad_gate = add(mine[0], came[0])[None]
    grad_up = add(mine[1], came[1])[None]
    grad_down = down_grad[None]
    return (grad_tokens, grad_weights.T, grad_gate, grad_up, grad_down)


def solution(mesh):
    spec = P(("dp", "expert"), None)
    weight = P("expert", None, None)
    out = P("expert", "dp", None)
    return jax.shard_map(
        local,
        mesh=mesh,
        in_specs=(spec, spec, spec, spec, weight, weight, weight),
        out_specs=(spec, spec, out, out, out),
        check_vma=False,
    )
```

```python
import functools

import jax
import jax.numpy as jnp
import numpy as np
from jax import lax
from jax.experimental import pallas as pl
from jax.experimental.pallas import tpu as pltpu
from jax.sharding import PartitionSpec as P

D = 3584
FF = 1024
TOP = 2
CAP = 64
EXPERTS = 8
ROWS = EXPERTS * CAP
TOK = 128
EXTRA = 128
WIDE = D + EXTRA
TILE = 1792
NT = D // TILE
NZ = 4
ZB = D // NZ
SUB = ZB // 4
HALF = FF // 2
BF = jnp.bfloat16
F32 = jnp.float32
FIRST = (((0,), (0,)), ((), ()))
LAST = (((1,), (1,)), ((), ()))
MB = 1 << 20


def params(limit=63):
    return pltpu.CompilerParams(vmem_limit_bytes=limit * MB + MB // 2)


def cost(flops, nbytes, trans=0):
    return pl.CostEstimate(flops=flops, bytes_accessed=nbytes, transcendentals=trans)


SHORT = cost(1, 1)
LONG = cost(40_000_000_000, 1)
PRODUCT = cost(16 * SUB * ROWS * FF, 8 * MB)
WIDE_COSTS = (PRODUCT, PRODUCT, cost(25_000_000_000, 1), SHORT)
SUMS = cost(10_000_000_000, 1)


def place_kernel(routes_ref, tokens_ref, picks_ref, out_ref):
    @pl.when(pl.program_id(0) == 0)
    def _():
        ids = lax.broadcasted_iota(jnp.int32, (EXPERTS, TOK), 0)
        named = [(routes_ref[k : k + 1, :] == ids).astype(F32) for k in range(TOP)]
        row = lax.broadcasted_iota(jnp.int32, (TOK, TOK), 0)
        col = lax.broadcasted_iota(jnp.int32, (TOK, TOK), 1)
        before = (row < col).astype(F32).astype(BF)
        rank = jnp.dot((named[0] + named[1]).astype(BF), before, preferred_element_type=F32)
        slot = lax.broadcasted_iota(jnp.int32, (CAP, TOK), 0).astype(F32)
        for k in range(TOP):
            for e in range(EXPERTS):
                hit = (slot == rank[e : e + 1, :]) & (named[k][e : e + 1, :] > 0.5)
                picks_ref[k, e * CAP : (e + 1) * CAP, :] = hit.astype(F32).astype(BF)

    both = picks_ref[0] + picks_ref[1]
    out_ref[...] = jnp.dot(both, tokens_ref[...], preferred_element_type=F32).astype(BF)


def place_tokens(routes, tokens):
    return pl.pallas_call(
        place_kernel,
        grid=(NT,),
        in_specs=[
            pl.BlockSpec((TOP, TOK), lambda i: (0, 0)),
            pl.BlockSpec((TOK, TILE), lambda i: (0, i)),
        ],
        out_specs=[
            pl.BlockSpec((TOP, ROWS, TOK), lambda i: (0, 0, 0)),
            pl.BlockSpec((ROWS, TILE), lambda i: (0, i)),
        ],
        out_shape=[
            jax.ShapeDtypeStruct((TOP, ROWS, TOK), BF),
            jax.ShapeDtypeStruct((ROWS, D), BF),
        ],
        compiler_params=params(),
        cost_estimate=cost(2 * ROWS * TOK * D, 5 * MB),
    )(routes.T, tokens)


def grads_kernel(picks_ref, probs_ref, grads_ref, out_ref):
    step = pl.program_id(0)

    @pl.when(step < NT)
    def _():
        both = picks_ref[0] + picks_ref[1]
        out_ref[...] = jnp.dot(both, grads_ref[...], preferred_element_type=F32).astype(BF)

    @pl.when(step == NT)
    def _():
        held = picks_ref[0] * probs_ref[0:1, :] + picks_ref[1] * probs_ref[1:2, :]
        ones = jnp.ones((TOK, EXTRA), BF)
        spread = jnp.dot(held, ones, preferred_element_type=F32)
        out_ref[:, :EXTRA] = spread.astype(BF)


def place_grads(picks, probs, grads):
    return pl.pallas_call(
        grads_kernel,
        grid=(NT + 1,),
        in_specs=[
            pl.BlockSpec((TOP, ROWS, TOK), lambda i: (0, 0, 0)),
            pl.BlockSpec((TOP, TOK), lambda i: (0, 0)),
            pl.BlockSpec((TOK, TILE), lambda i: (0, jnp.minimum(i, NT - 1))),
        ],
        out_specs=pl.BlockSpec((ROWS, TILE), lambda i: (0, i)),
        out_shape=jax.ShapeDtypeStruct((ROWS, WIDE), BF),
        compiler_params=params(),
        cost_estimate=cost(2 * ROWS * TOK * D, 5 * MB),
    )(picks, probs.T, grads)


def forward_kernel(x_ref, gate_ref, up_ref, hidden_ref, active_ref, slope_ref):
    x = x_ref[...]
    gate = jnp.dot(x, gate_ref[...], preferred_element_type=F32)
    up = jnp.dot(x, up_ref[...], preferred_element_type=F32)
    s = jax.nn.sigmoid(gate)
    active = gate * s
    hidden_ref[...] = (active * up).astype(BF)
    active_ref[...] = active
    slope_ref[...] = up * s * (1.0 + gate * (1.0 - s))


def forward(x, gate, up):
    n = 256
    return pl.pallas_call(
        forward_kernel,
        grid=(FF // n,),
        in_specs=[
            pl.BlockSpec((ROWS, D), lambda i: (0, 0)),
            pl.BlockSpec((D, n), lambda i: (0, i)),
            pl.BlockSpec((D, n), lambda i: (0, i)),
        ],
        out_specs=[pl.BlockSpec((ROWS, n), lambda i: (0, i))] * 3,
        out_shape=[
            jax.ShapeDtypeStruct((ROWS, FF), BF),
            jax.ShapeDtypeStruct((ROWS, FF), F32),
            jax.ShapeDtypeStruct((ROWS, FF), F32),
        ],
        compiler_params=params(),
        cost_estimate=cost(4 * ROWS * D * FF, 23 * MB, ROWS * FF),
    )(x, gate, up)


def backward_kernel(g_ref, down_ref, hidden_ref, active_ref, slope_ref, *refs):
    both_ref, wg_ref, total = refs[-3:]
    step = pl.program_id(0)
    back = jnp.dot(g_ref[:, :D], down_ref[...], preferred_element_type=F32)
    part = jnp.sum(back * hidden_ref[...].astype(F32), axis=1, keepdims=True)

    @pl.when(step == 0)
    def _():
        total[...] = jnp.zeros_like(total)

    total[...] += jnp.broadcast_to(part, total.shape)
    scaled = g_ref[:, D : D + 1].astype(F32) * back
    both_ref[0] = (scaled * slope_ref[...]).astype(BF)
    both_ref[1] = (scaled * active_ref[...]).astype(BF)
    wg_ref[...] = total[...].astype(BF)


def backward(g, down, hidden, active, slope, after=()):
    n = 512
    tile = pl.BlockSpec((ROWS, n), lambda i: (0, i))
    return pl.pallas_call(
        backward_kernel,
        grid=(FF // n,),
        in_specs=[
            pl.BlockSpec((ROWS, WIDE), lambda i: (0, 0)),
            pl.BlockSpec((D, n), lambda i: (0, i)),
            tile,
            tile,
            tile,
        ]
        + [pl.BlockSpec(memory_space=pl.ANY)] * len(after),
        out_specs=[
            pl.BlockSpec((2, ROWS, n), lambda i: (0, 0, i)),
            pl.BlockSpec((ROWS, EXTRA), lambda i: (0, 0)),
        ],
        out_shape=[
            jax.ShapeDtypeStruct((2, ROWS, FF), BF),
            jax.ShapeDtypeStruct((ROWS, EXTRA), BF),
        ],
        scratch_shapes=[pltpu.VMEM((ROWS, EXTRA), F32)],
        compiler_params=params(),
        cost_estimate=cost(2 * ROWS * D * FF, 18 * MB),
    )(g, down, hidden, active, slope, *after)


def rows_kernel(both_ref, gate_ref, up_ref, wg_ref, *refs):
    out_ref = refs[-1]
    step = pl.program_id(0)

    @pl.when(step < NT)
    def _():
        grad = lax.dot_general(both_ref[0], gate_ref[...], LAST, preferred_element_type=F32)
        grad = grad + lax.dot_general(both_ref[1], up_ref[...], LAST, preferred_element_type=F32)
        out_ref[...] = grad.astype(BF)

    @pl.when(step == NT)
    def _():
        out_ref[:, :EXTRA] = wg_ref[...]


def row_grads(both, gate, up, wg, after=()):
    clamp = lambda i: (jnp.minimum(i, NT - 1), 0)
    return pl.pallas_call(
        rows_kernel,
        grid=(NT + 1,),
        in_specs=[
            pl.BlockSpec((2, ROWS, FF), lambda i: (0, 0, 0)),
            pl.BlockSpec((TILE, FF), clamp),
            pl.BlockSpec((TILE, FF), clamp),
            pl.BlockSpec((ROWS, EXTRA), lambda i: (0, 0)),
        ]
        + [pl.BlockSpec(memory_space=pl.ANY)] * len(after),
        out_specs=pl.BlockSpec((ROWS, TILE), lambda i: (0, i)),
        out_shape=jax.ShapeDtypeStruct((ROWS, WIDE), BF),
        compiler_params=params(),
        cost_estimate=SHORT,
    )(both, gate, up, wg, *after)


def turned_kernel(scaled, deps, place_ref, x_ref, p_ref, *refs):
    send_ref, keep_ref, turned = refs[deps:]
    rows_in = x_ref[...]
    if scaled:
        rows_in = (p_ref[:, 0:1].astype(F32) * rows_in.astype(F32)).astype(BF)
    turned[...] = rows_in.T
    core, x = place_ref[8], place_ref[9]
    for j in range(2):
        rows = slice(j * SUB, (j + 1) * SUB)
        block = 2 * (x + j - 2 * x * j)
        far = pl.multiple_of((block + 1 - core) * SUB, SUB)
        near = pl.multiple_of((block + core) * SUB, SUB)
        send_ref[0, rows, :] = turned[pl.ds(far, SUB), :]
        keep_ref[0, rows, :] = turned[pl.ds(near, SUB), :]


def turned(place, x, p, scaled, after=()):
    last = (p.shape[1] // EXTRA) - 1
    send, keep = pl.pallas_call(
        functools.partial(turned_kernel, scaled, len(after)),
        grid_spec=pltpu.PrefetchScalarGridSpec(
            num_scalar_prefetch=1,
            grid=(NZ,),
            in_specs=[
                pl.BlockSpec((ROWS, ZB), lambda i, place: (0, i)),
                pl.BlockSpec((ROWS, EXTRA), lambda i, place: (0, last)),
            ]
            + [pl.BlockSpec(memory_space=pl.ANY)] * len(after),
            out_specs=[pl.BlockSpec((1, 2 * SUB, ROWS), lambda i, place: (i, 0, 0))] * 2,
            scratch_shapes=[pltpu.VMEM((ZB, ROWS), BF)],
        ),
        out_shape=[jax.ShapeDtypeStruct((NZ, 2 * SUB, ROWS), BF)] * 2,
        compiler_params=params(),
        cost_estimate=cost(ROWS * D, 8 * MB),
    )(place, x, p, *after)
    return keep, lax.ppermute(send, "dp", TO_CORE)


def combine_kernel(picks_ref, rows_ref, *refs):
    tokens_ref, weights_ref = refs[-2:]
    step = pl.program_id(0)

    @pl.when(step < NT)
    def _():
        both = picks_ref[0] + picks_ref[1]
        tokens_ref[...] = lax.dot_general(
            both, rows_ref[...], FIRST, preferred_element_type=F32
        ).astype(BF)

    @pl.when(step == NT)
    def _():
        for k in range(TOP):
            found = lax.dot_general(
                rows_ref[:, :EXTRA], picks_ref[k], FIRST, preferred_element_type=F32
            )
            weights_ref[k : k + 1, :] = found[0:1].astype(BF)


def combine(picks, rows, after=()):
    return pl.pallas_call(
        combine_kernel,
        grid=(NT + 1,),
        in_specs=[
            pl.BlockSpec((TOP, ROWS, TOK), lambda i: (0, 0, 0)),
            pl.BlockSpec((ROWS, TILE), lambda i: (0, i)),
        ]
        + [pl.BlockSpec(memory_space=pl.ANY)] * len(after),
        out_specs=[
            pl.BlockSpec((TOK, TILE), lambda i: (0, jnp.minimum(i, NT - 1))),
            pl.BlockSpec((TOP, TOK), lambda i: (0, 0)),
        ],
        out_shape=[
            jax.ShapeDtypeStruct((TOK, D), BF),
            jax.ShapeDtypeStruct((TOP, TOK), BF),
        ],
        compiler_params=params(),
        cost_estimate=SHORT,
    )(picks, rows, *after)


def moves(f):
    pairs = []
    for z in range(NZ):
        for x in range(2):
            for c in range(2):
                tz, tx, tc = f(z, x, c)
                pairs.append((z * 4 + x * 2 + c, (tz % NZ) * 4 + tx * 2 + tc))
    return pairs


TO_CORE = moves(lambda z, x, c: (z, x, 1 - c))
TO_UP = moves(lambda z, x, c: (z + 1, x, c))
TO_DOWN = moves(lambda z, x, c: (z - 1, x, c))
TO_TWO = moves(lambda z, x, c: (z + 2, x, c))
TO_X = moves(lambda z, x, c: (z, 1 - x, c))


def add(*parts):
    total = parts[0].astype(F32)
    for part in parts[1:]:
        total = total + part.astype(F32)
    return total.astype(BF)


def wide_kernel(place_ref, left_a, left_b, right_a, right_b, *refs):
    total = jnp.dot(left_a[0], right_a[0], preferred_element_type=F32)
    total = total + jnp.dot(left_b[0], right_b[0], preferred_element_type=F32)
    for k, out_ref in enumerate(refs[-2:]):

        @pl.when(pl.program_id(0) == k)
        def _():
            out_ref[...] = total.astype(BF)


def wide_parts(place, step, lefts, rights, after=()):
    left = pl.BlockSpec((1, 2 * SUB, ROWS), lambda i, place: (place[2 * step + i], 0, 0))
    right = pl.BlockSpec((1, ROWS, FF), lambda i, place: (i, 0, 0))
    return pl.pallas_call(
        wide_kernel,
        grid_spec=pltpu.PrefetchScalarGridSpec(
            num_scalar_prefetch=1,
            grid=(2,),
            in_specs=[left, left, right, right]
            + [pl.BlockSpec(memory_space=pl.ANY)] * len(after),
            out_specs=[pl.BlockSpec((2 * SUB, FF), lambda i, place: (0, 0))] * 2,
        ),
        out_shape=[jax.ShapeDtypeStruct((2 * SUB, FF), BF)] * 2,
        compiler_params=params(),
        cost_estimate=WIDE_COSTS[step],
    )(place, *lefts, *rights, *after)


def down_kernel(place_ref, left_a, left_b, right_a, right_b, *refs):
    far_ref, near_ref = refs[-2:]
    total = jnp.dot(left_a[0], right_a[...], preferred_element_type=F32)
    total = total + jnp.dot(left_b[0], right_b[...], preferred_element_type=F32)
    near_ref[0] = total[:SUB].astype(BF)
    far_ref[0] = total[SUB:].astype(BF)


def down_parts(place, lefts, rights, after=()):
    left = pl.BlockSpec((1, 2 * SUB, ROWS), lambda i, place: (place[i + 3 * (i // 3)], 0, 0))
    right = pl.BlockSpec((ROWS, FF), lambda i, place: (0, 0))
    return pl.pallas_call(
        down_kernel,
        grid_spec=pltpu.PrefetchScalarGridSpec(
            num_scalar_prefetch=1,
            grid=(NZ,),
            in_specs=[left, left, right, right]
            + [pl.BlockSpec(memory_space=pl.ANY)] * len(after),
            out_specs=[pl.BlockSpec((1, SUB, FF), lambda i, place: (i, 0, 0))] * 2,
        ),
        out_shape=[jax.ShapeDtypeStruct((NZ, SUB, FF), BF)] * 2,
        compiler_params=params(),
        cost_estimate=PRODUCT,
    )(place, *lefts, *rights, *after)


def around(up, down):
    return lax.ppermute(up, "dp", TO_UP), lax.ppermute(down, "dp", TO_DOWN)


def wide_add_kernel(part_up, part_down, up_ref, down_ref, *refs):
    refs[-2][...] = (part_up[...].astype(F32) + up_ref[...].astype(F32)).astype(BF)
    refs[-1][...] = (part_down[...].astype(F32) + down_ref[...].astype(F32)).astype(BF)


def wide_add(parts, moved, after=()):
    spec = pl.BlockSpec((SUB, FF), lambda i: (i, 0))
    return pl.pallas_call(
        wide_add_kernel,
        grid=(2,),
        in_specs=[spec] * 4 + [pl.BlockSpec(memory_space=pl.ANY)] * len(after),
        out_specs=[spec] * 2,
        out_shape=[jax.ShapeDtypeStruct((2 * SUB, FF), BF)] * 2,
        compiler_params=params(),
        cost_estimate=SHORT,
    )(*parts, *moved, *after)


def wide_away_kernel(part_up, part_down, up_ref, down_ref, *refs):
    for k, (a, b) in enumerate(((part_up, up_ref), (part_down, down_ref))):
        refs[-1][k] = (a[...].astype(F32) + b[...].astype(F32)).astype(BF)


def wide_away(parts, moved, after=()):
    half = SUB // 2
    spec = pl.BlockSpec((half, FF), lambda i: (2 + i, 0))
    return pl.pallas_call(
        wide_away_kernel,
        grid=(2,),
        in_specs=[spec] * 4 + [pl.BlockSpec(memory_space=pl.ANY)] * len(after),
        out_specs=pl.BlockSpec((2, half, FF), lambda i: (0, i, 0)),
        out_shape=jax.ShapeDtypeStruct((2, SUB, FF), BF),
        compiler_params=params(),
        cost_estimate=SHORT,
    )(*parts, *moved, *after)


def wide_end_kernel(part_up, part_down, up_ref, down_ref, came_ref, *refs):
    for k, (a, b) in enumerate(((part_up, up_ref), (part_down, down_ref))):
        total = a[...].astype(F32) + b[...].astype(F32) + came_ref[k].astype(F32)
        refs[-2 + k][...] = total.astype(BF)


def wide_end(parts, moved, came, after=()):
    half = SUB // 2
    spec = pl.BlockSpec((half, FF), lambda i: (i, 0))
    return pl.pallas_call(
        wide_end_kernel,
        grid=(2,),
        in_specs=[spec] * 4
        + [pl.BlockSpec((2, half, FF), lambda i: (0, i, 0))]
        + [pl.BlockSpec(memory_space=pl.ANY)] * len(after),
        out_specs=[spec] * 2,
        out_shape=[jax.ShapeDtypeStruct((SUB, FF), BF)] * 2,
        compiler_params=params(),
        cost_estimate=SHORT,
    )(*parts, *moved, came, *after)


def down_sums_kernel(near_ref, far_ref, *refs):
    for k, out_ref in enumerate(refs[-3:]):
        out_ref[...] = (near_ref[k].astype(F32) + far_ref[k].astype(F32)).astype(BF)


def down_sums(near, far, after=()):
    some = pl.BlockSpec((NZ - 1, SUB, FF), lambda i: (0, 0, 0))
    return pl.pallas_call(
        down_sums_kernel,
        grid=(1,),
        in_specs=[some] * 2 + [pl.BlockSpec(memory_space=pl.ANY)] * len(after),
        out_specs=[pl.BlockSpec((SUB, FF), lambda i: (0, 0))] * 3,
        out_shape=[jax.ShapeDtypeStruct((SUB, FF), BF)] * 3,
        compiler_params=params(),
        cost_estimate=SUMS,
    )(near, far, *after)


def down_last_kernel(near_ref, far_ref, a_ref, b_ref, c_ref, *refs):
    total = near_ref[0].astype(F32) + far_ref[0].astype(F32)
    for ref in (a_ref, b_ref, c_ref):
        total = total + ref[...].astype(F32)
    refs[-1][...] = total.astype(BF)


def down_last(near, far, came, after=()):
    half = SUB // 2
    own = pl.BlockSpec((1, half, FF), lambda i: (NZ - 1, i, 0))
    spec = pl.BlockSpec((half, FF), lambda i: (i, 0))
    return pl.pallas_call(
        down_last_kernel,
        grid=(2,),
        in_specs=[own] * 2 + [spec] * 3 + [pl.BlockSpec(memory_space=pl.ANY)] * len(after),
        out_specs=spec,
        out_shape=jax.ShapeDtypeStruct((SUB, FF), BF),
        compiler_params=params(),
        cost_estimate=LONG,
    )(near, far, *came, *after)


PLACES = np.array(
    [
        [v for s in range(NZ) for v in ((z - 1 - s) % NZ, (z + 1 + s) % NZ)] + [c, x]
        for z in range(NZ)
        for x in range(2)
        for c in range(2)
    ],
    np.int32,
)


def exchange(rows):
    width = rows.shape[1]
    out = lax.all_to_all(
        rows.reshape(EXPERTS, CAP, width), "expert", split_axis=0, concat_axis=0, tiled=True
    )
    return out.reshape(ROWS, width)


def local(tokens, grad_out, routes, probs, w_gate, w_up, w_down):
    place = lax.dynamic_slice(PLACES.reshape(-1), (10 * lax.axis_index("dp"),), (10,))
    gate, up, down = w_gate[0], w_up[0], w_down[0]
    picks, send_tokens = place_tokens(routes, tokens)
    row_tokens = exchange(send_tokens)
    send_grads = place_grads(picks, probs, grad_out)
    row_grads_in = exchange(send_grads)
    hidden, active, slope = forward(row_tokens, gate, up)
    lefts = turned(place, row_tokens, row_tokens, False, after=(hidden,))
    hiddens = (hidden, lax.ppermute(hidden, "dp", TO_CORE))
    both, wg = backward(
        row_grads_in, down, hidden, active, slope, after=(lefts[0], lefts[1], hiddens[1])
    )
    boths = (both, lax.ppermute(both, "dp", TO_CORE))
    dlefts = turned(place, row_grads_in, row_grads_in, True, after=(both,))
    ring0 = wide_parts(place, 0, lefts, boths, after=dlefts[:1])
    moved0 = around(*ring0)
    far, near = down_parts(place, dlefts, hiddens, after=ring0[:1])
    far_in = lax.ppermute(far, "dp", TO_X)
    parts1 = wide_parts(place, 1, lefts, boths, after=(far,))
    ring1 = wide_add(parts1, moved0)
    moved1 = around(*ring1)
    sent_rows = row_grads(both, gate, up, wg, after=ring1)
    returned = exchange(sent_rows)
    parts2 = wide_parts(place, 2, lefts, boths, after=(sent_rows,))
    ring2 = wide_add(parts2, moved1)
    moved2 = around(*ring2)
    parts3 = wide_parts(place, 3, lefts, boths, after=ring2)
    sums = down_sums(near, far_in, after=parts3)
    ways = (TO_DOWN, TO_UP, TO_TWO)
    down_came = [lax.ppermute(part, "dp", way) for part, way in zip(sums, ways)]
    away = wide_away(parts3, moved2, after=sums)
    came = lax.ppermute(away, "dp", TO_X)
    grad_tokens, grad_weights = combine(picks, returned, after=(away,))
    down_grad = down_last(near, far_in, down_came, after=(grad_tokens,))
    gate_grad, up_grad = wide_end(parts3, moved2, came, after=(down_grad,))
    grad_gate, grad_up = gate_grad[None], up_grad[None]
    grad_down = down_grad[None]
    return (grad_tokens, grad_weights.T, grad_gate, grad_up, grad_down)


def solution(mesh):
    spec = P(("dp", "expert"), None)
    weight = P("expert", None, None)
    out = P("expert", "dp", None)
    return jax.shard_map(
        local,
        mesh=mesh,
        in_specs=(spec, spec, spec, spec, weight, weight, weight),
        out_specs=(spec, spec, out, out, out),
        check_vma=False,
    )
```
